32 devices in a mesh: row: 4 (over z), col: 4 (over y, x), ch: 2 (over core).
Axes of the slice: x: 2, y: 2, z: 4, core: 2. Of those that a mesh axis runs over, the one named last changes fastest.
Arguments:
- field: float32 [32, 512, 2048], P(None, 'row', 'col'), may hold values from -6 to 6
- spec_weight: float32 [2, 32, 32, 512], replicated, may hold values from -0.75 to 0.75
- point_weight: float32 [32, 32], replicated, may hold values from -1 to 1
- bias: float32 [32], P('ch'), may hold values from -1 to 1
- kept_modes: int32 [32], replicated, may hold values from 8 to 16, as said below
- residual: float32 [32, 16384], P('ch', ('row', 'col')), may hold values from -6 to 6
- trace_dest: int32 [16384, 1], P(('row', 'col')), may hold values from 0 to 15; in each aligned block of 1024 rows (0 to 1023, 1024 to 2047, ...) at most 128 rows name the same one
- trace_cell: int32 [16384], P(('row', 'col')), may hold values from 0 to 65535
Outputs:
- grad_field: float32 [32, 512, 2048], P('ch', 'row', 'col')
- grad_spec: float32 [2, 32, 32, 512], P(None, None, 'ch')
- grad_point: float32 [32, 32], P(None, 'ch')
- grad_bias: float32 [32], P('ch')
The draws below stay inside these ranges and needn't reach their ends.
Inputs may be any that keep to these rules, and one draw needn't show every extreme that they name: `trace_dest`: of the 1024 points of one device, at most 128 go to one tile. `kept_modes`: some channel keeps 16 and some keeps 16 // 2.
All inputs are finite; a program needn't handle non-finite values.
Results may differ from the reference program's by a relative error of at most 0.00012.
Values sent between devices are 32-bit elements; how exact they have to be, the bound alone decides.
A program may use at most 192 MiB of HBM per device.

```python
import math
import jax
import jax.numpy as jnp
import numpy as np
from jax import lax

C = 32
M = 16
RD = 128
CD = 512
P_DEV = 1024
NR = 512
NC = 2048
TILES = 16
NPTS = 16384
MODES = 512
CAP = 128
N_COL = 4


def draw_kept_modes(key, part):
    values = jax.random.randint(key, (C,), M // 2, M + 1)
    first_spot = jax.random.randint(jax.random.fold_in(key, 11), (), 0, C)
    shift_by = jax.random.randint(jax.random.fold_in(key, 13), (), 1, C)
    second_spot = (first_spot + shift_by) % C
    places = jnp.arange(C)
    values = jnp.where(places == first_spot, M, values)
    values = jnp.where(places == second_spot, M // 2, values)
    return values.astype(jnp.int32)


def set_ends(drawn, stream_key, low, top_value):
    place = [jax.random.randint(jax.random.fold_in(stream_key, axis), (), 0, length) for axis, length in enumerate(drawn.shape)]
    main_axis = drawn.shape.index(max(drawn.shape))
    next_to = place[:main_axis] + [(place[main_axis] + 1) % drawn.shape[main_axis]] + place[main_axis + 1:]
    return drawn.at[tuple(place)].set(low).at[tuple(next_to)].set(top_value)


def shard_levels(stream_key, shape, pieces, least, top_value):
    level = 1.0
    for position, blocks in pieces:
        heights = jax.random.uniform(jax.random.fold_in(jax.random.fold_in(stream_key, 6), position), (blocks,), jnp.float32, least / len(pieces), top_value / len(pieces))
        level = level * jnp.repeat(jnp.exp(heights), shape[position] // blocks).reshape((-1,) + (1,) * (len(shape) - 1 - position))
    return level


def assign_block(stream_key, own, number, rows, count, top, bound, skew):
    sequence = jax.random.permutation(stream_key, count)
    packed, usual = portions_of(count, rows * top, bound, skew, True), portions_of(count, rows * top, bound, skew, False)
    places = jnp.arange(count)

    def named(tallies, turn):
        used = int((tallies > 0).sum())
        fixed = max(1, used // 4)
        shifted = fixed + (places - fixed + turn * (used - fixed)) % max(1, count - fixed)
        return jnp.zeros((count,), jnp.int32).at[sequence[jnp.where(places < fixed, places, shifted)]].set(jnp.asarray(tallies, jnp.int32))

    tallies = jnp.where(number % 4 == 0, named(packed, number // 4), named(usual, number - number // 4 - 1))
    mixed = jax.random.permutation(jax.random.fold_in(own, 3), count)
    giver, taker = mixed[0:count // 2 * 2:2], mixed[1:count // 2 * 2:2]
    room = jnp.minimum(tallies[giver] - 1, bound - tallies[taker]) // 2
    room = jnp.where((giver == sequence[0]) | (taker == sequence[0]) | (tallies[taker] == 0), 0, jnp.maximum(room, 0))
    shifted = jax.random.randint(jax.random.fold_in(own, 4), (count // 2,), 0, 1 << 20) % (room + 1)
    tallies = tallies.at[giver].add(-shifted).at[taker].add(shifted)
    labels = jnp.searchsorted(jnp.cumsum(tallies), jnp.arange(rows * top), side="right").astype(jnp.int32)
    table = labels.reshape(top, rows).T
    table = table[jax.random.permutation(jax.random.fold_in(own, 1), rows)]
    turn = jax.random.randint(jax.random.fold_in(own, 2), (rows, 1), 0, top)
    return jnp.take_along_axis(table, (jnp.arange(top)[None, :] + turn) % top, axis=1)


def portions_of(amount, total, bound, skew, full):
    portions = [(1 << 20) // math.isqrt(rank ** skew) + 1 for rank in range(1, amount + 1)]
    largest = bound if full else min(bound, max(-(-total // amount), total * portions[0] // sum(portions)))
    least = 1 if total - largest >= amount - 1 else 0
    given, spare = [largest] + [least] * (amount - 1), total - largest - least * (amount - 1)
    while spare > 0:
        free = [i for i in range(1, amount) if given[i] < largest] or [i for i in range(1, amount) if given[i] < bound]
        pool, budget = sum([portions[i] for i in free]), spare
        for i in free:
            more = min(bound - given[i], max(1, budget * portions[i] // pool), spare)
            given[i] = given[i] + more
            spare = spare - more
    return np.array(given)


def scatter_about(rng, dims, spread, limit, split=(), kind=jnp.bfloat16):
    values = spread * jax.random.normal(rng, dims, jnp.float32)
    if split:
        values = values * shard_levels(rng, dims, split, -0.22, 0.18)
    return jnp.clip(values, -limit, limit).astype(kind)


def setup_inputs(seed: int = 0) -> dict:
    splits = jax.random.split(jax.random.key(seed), 9)
    field = scatter_about(splits[0], (C, NR, NC), 1.0, 6.0, ((1, 4), (2, 4)), jnp.float32)
    spec_weight = scatter_about(splits[1], (2, C, C, MODES), (2 * C) ** -0.5, 0.75, (), jnp.float32)
    point_weight = scatter_about(splits[2], (C, C), C ** -0.5, 1.0, (), jnp.float32)
    bias = jnp.clip(jax.random.uniform(splits[3], (C,), jnp.float32, -1.0, 1.0) * shard_levels(splits[3], (C,), ((0, 2),), -0.4, 0.0), -1.0, 1.0)
    kept_modes = draw_kept_modes(jax.random.fold_in(splits[8], 71), 0)
    residual = scatter_about(splits[5], (C, NPTS), 1.0, 6.0, ((0, 2), (1, 16)), jnp.float32)
    trace_dest_keys = jax.random.split(jax.random.fold_in(splits[6], 1), NPTS // P_DEV)
    trace_dest_turns = jax.random.permutation(jax.random.fold_in(splits[6], 3), NPTS // P_DEV)
    trace_dest = jax.vmap(lambda own, number: assign_block(jax.random.fold_in(splits[6], 2), own, number, P_DEV, TILES, 1, CAP, 2))(trace_dest_keys, trace_dest_turns).reshape((NPTS, 1))
    trace_cell = set_ends(jax.random.randint(splits[7], (NPTS,), 0, RD * CD), jax.random.fold_in(splits[7], 1), 0, (RD * CD) - 1).astype(jnp.int32)
    return dict(field=field, spec_weight=spec_weight, point_weight=point_weight, bias=bias, kept_modes=kept_modes, residual=residual, trace_dest=trace_dest, trace_cell=trace_cell)


full_turn = 6.283185307179586
exact_mode = lax.Precision.HIGHEST

def row_angles(start_at, extent, period):
    frequency = jnp.arange(2 * M, dtype=jnp.int32)
    frequency = jnp.where(frequency < M, frequency, frequency - 2 * M)
    places = start_at + jnp.arange(extent, dtype=jnp.int32)
    phases = frequency[:, None] * places[None, :] % period
    angles = phases.astype(jnp.float32) * (full_turn / period)
    return (jnp.cos(angles), jnp.sin(angles))

def col_angles(start_at, extent, period):
    frequency = jnp.arange(M, dtype=jnp.int32)
    places = start_at + jnp.arange(extent, dtype=jnp.int32)
    phases = places[:, None] * frequency[None, :] % period
    angles = phases.astype(jnp.float32) * (full_turn / period)
    return (jnp.cos(angles), jnp.sin(angles))

def mode_mask(kept_modes):
    indices = jnp.arange(MODES, dtype=jnp.int32)
    row_mode = indices // M
    col_mode = indices % M
    row_rank = jnp.where(row_mode < M, row_mode, 2 * M - 1 - row_mode)
    allowed = (row_rank[None, :] < kept_modes[:, None]) & (col_mode[None, :] < kept_modes[:, None])
    return allowed.astype(jnp.float32)

def full_modes(values, scale_by):
    cos_rows, sin_rows = row_angles(0, NR, NR)
    real_rows = jnp.einsum('ar,crs->cas', cos_rows, values, precision=exact_mode)
    imag_rows = -jnp.einsum('ar,crs->cas', sin_rows, values, precision=exact_mode)
    cos_cols, sin_cols = col_angles(0, NC, NC)
    mode_re = jnp.einsum('cas,sb->cab', real_rows, cos_cols, precision=exact_mode) + jnp.einsum('cas,sb->cab', imag_rows, sin_cols, precision=exact_mode)
    mode_im = jnp.einsum('cas,sb->cab', imag_rows, cos_cols, precision=exact_mode) - jnp.einsum('cas,sb->cab', real_rows, sin_cols, precision=exact_mode)
    count = values.shape[0]
    return (mode_re.reshape(count, MODES) * scale_by, mode_im.reshape(count, MODES) * scale_by)

def full_field(mode_re, mode_im, scale_by):
    count = mode_re.shape[0]
    grid_re = mode_re.reshape(count, 2 * M, M)
    grid_im = mode_im.reshape(count, 2 * M, M)
    cos_cols, sin_cols = col_angles(0, NC, NC)
    half_re = jnp.einsum('cab,sb->cas', grid_re, cos_cols, precision=exact_mode) - jnp.einsum('cab,sb->cas', grid_im, sin_cols, precision=exact_mode)
    half_im = jnp.einsum('cab,sb->cas', grid_re, sin_cols, precision=exact_mode) + jnp.einsum('cab,sb->cas', grid_im, cos_cols, precision=exact_mode)
    cos_rows, sin_rows = row_angles(0, NR, NR)
    result = jnp.einsum('ar,cas->crs', cos_rows, half_re, precision=exact_mode) - jnp.einsum('ar,cas->crs', sin_rows, half_im, precision=exact_mode)
    return result * scale_by

def reference(field, spec_weight, point_weight, bias, kept_modes, residual, trace_dest, trace_cell):
    forward_scale = 1.0 / math.sqrt(NR * NC)
    mix_scale = 1.0 / math.sqrt(MODES)
    spec_re, spec_im = full_modes(field, forward_scale)
    allowed = mode_mask(kept_modes)
    weight_re = spec_weight[0] * allowed[None, :, :]
    weight_im = spec_weight[1] * allowed[None, :, :]
    mixed_re = lax.optimization_barrier(jnp.sum(weight_re * spec_re[:, None, :] - weight_im * spec_im[:, None, :], axis=0))
    mixed_im = lax.optimization_barrier(jnp.sum(weight_re * spec_im[:, None, :] + weight_im * spec_re[:, None, :], axis=0))
    pre_act = full_field(mixed_re, mixed_im, mix_scale) + jnp.einsum('co,crs->ors', point_weight, field, precision=exact_mode) + bias[:, None, None]
    targets = trace_dest[:, 0]
    rows_at = targets // N_COL * RD + trace_cell // CD
    cols_at = targets % N_COL * CD + trace_cell % CD
    flat_cells = (rows_at * NC + cols_at).astype(jnp.int32)
    cotangent = jnp.zeros((C, NR * NC), jnp.float32).at[:, flat_cells].add(residual).reshape(C, NR, NC)
    slope = jax.vjp(jax.nn.gelu, pre_act)[1](cotangent)[0]
    grad_re, grad_im = full_modes(slope, mix_scale)
    grad_scale = math.sqrt(MODES / NPTS)
    spec_grad_re = allowed[None] * (grad_re[None] * spec_re[:, None] + grad_im[None] * spec_im[:, None]) * grad_scale
    spec_grad_im = allowed[None] * (grad_im[None] * spec_re[:, None] - grad_re[None] * spec_im[:, None]) * grad_scale
    grad_spec = jnp.stack((spec_grad_re, spec_grad_im), axis=0)
    adjoint_re = lax.optimization_barrier(jnp.sum(weight_re * grad_re[None] + weight_im * grad_im[None], axis=1))
    adjoint_im = lax.optimization_barrier(jnp.sum(weight_re * grad_im[None] - weight_im * grad_re[None], axis=1))
    grad_field = jnp.einsum('co,ors->crs', point_weight, slope, precision=exact_mode) + full_field(adjoint_re, adjoint_im, forward_scale)
    norm_points = 1.0 / math.sqrt(NPTS)
    grad_point = jnp.einsum('crs,ors->co', field, slope, precision=exact_mode) * norm_points
    grad_bias = lax.optimization_barrier(jnp.sum(slope, axis=(1, 2))) * norm_points
    return (grad_field, grad_spec, grad_point, grad_bias)
```

```python
import functools
import math

import jax
import jax.numpy as jnp
from jax import lax
from jax.experimental import pallas as pl
from jax.experimental.pallas import tpu as pltpu
from jax.sharding import PartitionSpec as P

M = 16
A = 2 * M
MODES = A * M
RB = 8
F32 = jnp.float32
BF16 = jnp.bfloat16
FULL_TURN = 6.283185307179586
NN = (((1,), (0,)), ((), ()))
NT = (((1,), (1,)), ((), ()))
MIB = 1 << 20


def row_table(start_at, extent, period):
    frequency = jnp.arange(A, dtype=jnp.int32)
    frequency = jnp.where(frequency < M, frequency, frequency - A)
    places = start_at + jnp.arange(extent, dtype=jnp.int32)
    phases = frequency[:, None] * places[None, :] % period
    angles = phases.astype(F32) * (FULL_TURN / period)
    return jnp.concatenate((jnp.cos(angles), jnp.sin(angles)), axis=0)


def col_table(start_at, extent, period):
    frequency = jnp.arange(M, dtype=jnp.int32)
    places = start_at + jnp.arange(extent, dtype=jnp.int32)
    phases = frequency[:, None] * places[None, :] % period
    angles = phases.astype(F32) * (FULL_TURN / period)
    return jnp.concatenate((jnp.cos(angles), jnp.sin(angles)), axis=0)


def mode_mask(kept_modes):
    indices = jnp.arange(MODES, dtype=jnp.int32)
    row_mode = indices // M
    col_mode = indices % M
    row_rank = jnp.where(row_mode < M, row_mode, 2 * M - 1 - row_mode)
    allowed = (row_rank[None, :] < kept_modes[:, None]) & (col_mode[None, :] < kept_modes[:, None])
    return allowed.astype(F32)


def split2(x):
    hi = x.astype(BF16)
    return hi, (x - hi.astype(F32)).astype(BF16)


def mm(a, b, dims=NN):
    return lax.dot_general(a, b, dims, preferred_element_type=F32)


def dot3(a, b, dims=NN):
    return mm(a[0], b[0], dims) + (mm(a[0], b[1], dims) + mm(a[1], b[0], dims))


def pack_kernel(tiles, cap, dest_ref, vals_ref, out_ref):
    n = dest_ref.shape[0]
    dest = dest_ref[...]
    wide = max(tiles, 128)
    named = dest == lax.broadcasted_iota(jnp.int32, (n, wide), 1)
    one_hot = named.astype(F32).astype(BF16)
    before = (
        lax.broadcasted_iota(jnp.int32, (n, n), 1) < lax.broadcasted_iota(jnp.int32, (n, n), 0)
    )
    earlier = mm(before.astype(F32).astype(BF16), one_hot)
    rank = jnp.sum(jnp.where(named, earlier, 0.0), axis=1, keepdims=True)
    position = dest * cap + rank.astype(jnp.int32)
    vals = vals_ref[...]
    rows = vals.shape[0]
    hi = vals.astype(BF16)
    left = vals - hi.astype(F32)
    mid = left.astype(BF16)
    low = (left - mid.astype(F32)).astype(BF16)
    parts = jnp.concatenate((hi.astype(F32), mid.astype(F32), low.astype(F32)), axis=0).astype(BF16)
    step = 512
    for first in range(0, tiles * cap, step):
        at = lax.broadcasted_iota(jnp.int32, (n, step), 1) + first
        place = (position == at).astype(F32).astype(BF16)
        got = mm(parts, place)
        out_ref[:, first : first + step] = (
            got[:rows] + got[rows : 2 * rows] + got[2 * rows : 3 * rows]
        )


def pack_points(dest, vals, tiles, cap):
    return pl.pallas_call(
        functools.partial(pack_kernel, tiles, cap),
        out_shape=jax.ShapeDtypeStruct((vals.shape[0], tiles * cap), F32),
        compiler_params=pltpu.CompilerParams(vmem_limit_bytes=40 * MIB),
    )(dest, vals)


def to_modes(rows2, tall, out_ref, at, scale):
    grid = dot3(rows2, split2(tall))
    out_ref[at, 0] = (grid[:A, :M] - grid[A:, M:]) * scale
    out_ref[at, 1] = (grid[A:, :M] + grid[:A, M:]) * (-scale)


def field_modes_kernel(scale, own_ref, field_ref, cols_ref, rows_ref, out_ref):
    count, height, width = field_ref.shape
    cols2 = split2(cols_ref[...])
    rows2 = split2(rows_ref[...])
    tall = dot3(split2(field_ref[...].reshape(count * height, width)), cols2)
    for c in range(count):
        to_modes(rows2, tall[c * height : (c + 1) * height], out_ref, c, scale)


def field_modes(field, own, own_count, cols, rows, scale):
    _, height, width = field.shape
    count = 4
    steps = own_count // count
    return pl.pallas_call(
        functools.partial(field_modes_kernel, scale),
        grid_spec=pltpu.PrefetchScalarGridSpec(
            num_scalar_prefetch=1,
            grid=(steps,),
            in_specs=[
                pl.BlockSpec((count, height, width), lambda i, own: (own[0] * steps + i, 0, 0)),
                pl.BlockSpec(cols.shape, lambda i, own: (0, 0)),
                pl.BlockSpec(rows.shape, lambda i, own: (0, 0)),
            ],
            out_specs=pl.BlockSpec((count, 2, A, M), lambda i, own: (i, 0, 0, 0)),
        ),
        out_shape=jax.ShapeDtypeStruct((own_count, 2, A, M), F32),
        compiler_params=pltpu.CompilerParams(vmem_limit_bytes=40 * MIB),
    )(own, field, cols, rows)


def slope_kernel(
    scale, field_ref, grid_ref, tall_rows_ref, wide_cols_ref, tall_cols_ref, rows_ref, kron_ref,
    bias_ref, vals_ref, rowid_ref, colid_ref, group_ref,
    slope_ref, modes_ref, point_ref,
    half_ref, hot_ref, vhi_ref, vlo_ref, tall_ref, acc_ref,
):
    step = pl.program_id(0)
    channels, _, width = slope_ref.shape
    rows = channels * RB
    points = vals_ref.shape[1]
    inputs = field_ref.shape[0]

    @pl.when(step == 0)
    def _():
        tall_rows = split2(tall_rows_ref[...])
        for o in range(channels):
            half_ref[o] = dot3(tall_rows, split2(grid_ref[o]))
        vals = vals_ref[...]
        hi = vals.astype(BF16).astype(F32)
        low = vals - hi
        vhi_ref[...] = jnp.broadcast_to(hi[:, None, :], (channels, RB, points)).reshape(rows, points)
        vlo_ref[...] = jnp.broadcast_to(low[:, None, :], (channels, RB, points)).reshape(rows, points)
        part = 256
        for first in range(0, points, part):
            ids = colid_ref[first : first + part, :]
            hot = ids == lax.broadcasted_iota(jnp.int32, (part, width), 1)
            hot_ref[first : first + part, :] = hot.astype(F32).astype(BF16)
        acc_ref[...] = jnp.zeros_like(acc_ref)

    block2 = split2(field_ref[...].reshape(inputs * RB, width))
    half = half_ref[:, pl.ds(pl.multiple_of(step * RB, RB), RB), :].reshape(rows, 2 * M)
    pre = (
        dot3(split2(half), split2(wide_cols_ref[...]))
        + dot3(split2(kron_ref[...]), block2)
        + bias_ref[...]
    )
    here = rowid_ref[...] == step * RB + lax.broadcasted_iota(jnp.int32, (RB, points), 0)
    here = jnp.broadcast_to(here.astype(F32)[None], (channels, RB, points)).reshape(rows, points)
    cot = mm((vhi_ref[...] * here).astype(BF16), hot_ref[...]) + mm(
        (vlo_ref[...] * here).astype(BF16), hot_ref[...]
    )
    k = math.sqrt(2.0 / math.pi)
    square = pre * pre
    t = jnp.tanh(k * pre * (1.0 + 0.044715 * square))
    rate = 0.5 * (1.0 + t) + 0.5 * k * pre * (1.0 - t * t) * (1.0 + 3 * 0.044715 * square)
    slope = cot * rate
    slope_ref[...] = slope.reshape(channels, RB, width)
    slope2 = split2(slope)
    tall = dot3(slope2, split2(tall_cols_ref[...]))
    tall_ref[:, pl.ds(pl.multiple_of(step * RB, RB), RB), :] = tall.reshape(channels, RB, 2 * M)
    acc_ref[...] += dot3(block2, slope2, NT)

    @pl.when(step == pl.num_programs(0) - 1)
    def _():
        rows2 = split2(rows_ref[...])
        for o in range(channels):
            to_modes(rows2, tall_ref[o], modes_ref, o, scale)
        total = acc_ref[...]
        same = lax.broadcasted_iota(jnp.int32, total.shape, 0) % RB == (
            lax.broadcasted_iota(jnp.int32, total.shape, 1) % RB
        )
        kept = jnp.sum(jnp.where(same, total, 0.0).reshape(inputs, RB, rows), axis=1)
        point_ref[...] = lax.dot_general(
            kept, group_ref[...], NN, precision=lax.Precision.HIGHEST, preferred_element_type=F32
        )


def whole(shape):
    return pl.BlockSpec(shape, lambda i: (0,) * len(shape))


def slope_pass(field, grid, wide_cols, cols_t, rows, rows_t, kron, bias, vals, rowid, colid, scale):
    inputs, height, width = field.shape
    channels = grid.shape[0]
    points = vals.shape[1]
    lanes = channels * RB
    group = (
        jnp.arange(lanes, dtype=jnp.int32)[:, None] // RB
        == jnp.arange(channels, dtype=jnp.int32)[None, :]
    ).astype(F32)
    args = (field, grid, rows_t, wide_cols, cols_t, rows, kron, bias, vals, rowid, colid, group)
    return pl.pallas_call(
        functools.partial(slope_kernel, scale),
        grid=(height // RB,),
        in_specs=[pl.BlockSpec((inputs, RB, width), lambda i: (0, i, 0))]
        + [whole(arg.shape) for arg in args[1:]],
        out_specs=[
            pl.BlockSpec((channels, RB, width), lambda i: (0, i, 0)),
            whole((channels, 2, A, M)),
            whole((inputs, channels)),
        ],
        out_shape=[
            jax.ShapeDtypeStruct((channels, height, width), F32),
            jax.ShapeDtypeStruct((channels, 2, A, M), F32),
            jax.ShapeDtypeStruct((inputs, channels), F32),
        ],
        scratch_shapes=[
            pltpu.VMEM((channels, height, 2 * M), F32),
            pltpu.VMEM((points, width), BF16),
            pltpu.VMEM((lanes, points), F32),
            pltpu.VMEM((lanes, points), F32),
            pltpu.VMEM((channels, height, 2 * M), F32),
            pltpu.VMEM((inputs * RB, lanes), F32),
        ],
        compiler_params=pltpu.CompilerParams(vmem_limit_bytes=52 * MIB),
    )(*args)


def back_kernel(
    own_ref, other_ref, grid_ref, tall_rows_ref, wide_cols_ref, kron_own_ref, kron_other_ref,
    out_ref, half_ref,
):
    step = pl.program_id(0)
    channels, block, width = out_ref.shape
    rows = channels * RB

    @pl.when(step == 0)
    def _():
        tall_rows = split2(tall_rows_ref[...])
        for c in range(channels):
            half_ref[c] = dot3(tall_rows, split2(grid_ref[c]))

    half = half_ref[:, pl.ds(pl.multiple_of(step * RB, RB), RB), :].reshape(rows, 2 * M)
    result = (
        dot3(split2(half), split2(wide_cols_ref[...]))
        + dot3(split2(kron_own_ref[...]), split2(own_ref[...].reshape(rows, width)))
        + dot3(split2(kron_other_ref[...]), split2(other_ref[...].reshape(rows, width)))
    )
    out_ref[...] = result.reshape(channels, RB, width)


def back_pass(own, other, grid, rows_t, wide_cols, kron_own, kron_other):
    channels, height, width = own.shape
    args = (own, other, grid, rows_t, wide_cols, kron_own, kron_other)
    block = pl.BlockSpec((channels, RB, width), lambda i: (0, i, 0))
    return pl.pallas_call(
        back_kernel,
        grid=(height // RB,),
        in_specs=[block, block] + [whole(arg.shape) for arg in args[2:]],
        out_specs=block,
        out_shape=jax.ShapeDtypeStruct((channels, height, width), F32),
        scratch_shapes=[pltpu.VMEM((channels, height, 2 * M), F32)],
        compiler_params=pltpu.CompilerParams(vmem_limit_bytes=40 * MIB),
    )(*args)


def sum_kernel(n_row, n_col, x_ref, out_ref, landed, total, gathered, send1, recv1, send2, recv2):
    n = n_row * n_col
    row = lax.axis_index("row")
    col = lax.axis_index("col")
    ch = lax.axis_index("ch")
    me = row * n_col + col

    def device(offset, flip):
        at = lax.rem(me + offset, n)
        return (at // n_col, lax.rem(at, n_col), lax.rem(ch + flip, 2))

    barrier = pltpu.get_barrier_semaphore()

    def greet(i, carry):
        pl.semaphore_signal(
            barrier, inc=1, device_id=device(i // 2, lax.rem(i, 2)),
            device_id_type=pl.DeviceIdType.MESH,
        )
        return carry

    lax.fori_loop(1, 2 * n, greet, 0)
    pl.semaphore_wait(barrier, 2 * n - 1)

    def scatter(k):
        return pltpu.make_async_remote_copy(
            src_ref=x_ref.at[lax.rem(me + k, n)],
            dst_ref=landed.at[k],
            send_sem=send1.at[k],
            recv_sem=recv1.at[k],
            device_id=device(k, 0),
            device_id_type=pl.DeviceIdType.MESH,
        )

    def start1(k, carry):
        scatter(k).start()
        return carry

    lax.fori_loop(1, n, start1, 0)
    total[...] = x_ref[me]

    def take(k, carry):
        scatter(k).wait_recv()
        total[...] += landed[k]
        return carry

    lax.fori_loop(1, n, take, 0)
    gathered[ch * n + me] = total[...]

    def spread(i):
        return pltpu.make_async_remote_copy(
            src_ref=total,
            dst_ref=gathered.at[ch * n + me],
            send_sem=send2.at[i],
            recv_sem=recv2.at[i],
            device_id=device(i // 2, lax.rem(i, 2)),
            device_id_type=pl.DeviceIdType.MESH,
        )

    def start2(i, carry):
        spread(i).start()
        return carry

    lax.fori_loop(1, 2 * n, start2, 0)

    def end1(k, carry):
        scatter(k).wait_send()
        return carry

    lax.fori_loop(1, n, end1, 0)

    def end2(i, carry):
        spread(i).wait()
        return carry

    lax.fori_loop(1, 2 * n, end2, 0)
    out_ref[...] = gathered[...]


def device_sum(x, n_row, n_col, which):
    n = n_row * n_col
    size = x.shape[0]
    tall = -(-size // (n * 128))
    x = jnp.pad(x, (0, n * tall * 128 - size)).reshape(n, tall, 128)
    out = pl.pallas_call(
        functools.partial(sum_kernel, n_row, n_col),
        out_shape=jax.ShapeDtypeStruct((2 * n, tall, 128), F32),
        in_specs=[pl.BlockSpec(memory_space=pltpu.VMEM)],
        out_specs=pl.BlockSpec(memory_space=pltpu.VMEM),
        scratch_shapes=[
            pltpu.VMEM((n, tall, 128), F32),
            pltpu.VMEM((tall, 128), F32),
            pltpu.VMEM((2 * n, tall, 128), F32),
            pltpu.SemaphoreType.DMA((n,)),
            pltpu.SemaphoreType.DMA((n,)),
            pltpu.SemaphoreType.DMA((2 * n,)),
            pltpu.SemaphoreType.DMA((2 * n,)),
        ],
        compiler_params=pltpu.CompilerParams(collective_id=which, has_side_effects=True),
    )(x)
    return out.reshape(2, n * tall * 128)[:, :size]


def mode_grid(re, im):
    count = re.shape[0]
    re = re.reshape(count, A, M)
    im = im.reshape(count, A, M)
    return jnp.concatenate(
        (jnp.concatenate((re, im), axis=2), jnp.concatenate((-im, re), axis=2)), axis=1
    )


def spread_rows(weights):
    eye = jnp.eye(RB, dtype=F32)
    a, b = weights.shape
    return (weights[:, None, :, None] * eye[None, :, None, :]).reshape(a * RB, b * RB)


def per_device(
    field, spec_weight, point_weight, bias, kept_modes, residual, trace_dest, trace_cell
):
    n_row = lax.axis_size("row")
    n_col = lax.axis_size("col")
    ch = lax.axis_index("ch")
    inputs, height, width = field.shape
    own = inputs // lax.axis_size("ch")
    first = ch * own
    points = trace_dest.shape[0]
    tiles = n_row * n_col
    points_all = points * tiles
    cap = max(2, 2 * points // tiles)
    forward_scale = 1.0 / math.sqrt(height * n_row * width * n_col)
    mix_scale = 1.0 / math.sqrt(MODES)

    rows = row_table(lax.axis_index("row") * height, height, height * n_row)
    cols = col_table(lax.axis_index("col") * width, width, width * n_col)
    rows_t = rows.T
    cols_t = cols.T
    wide_cols = jnp.concatenate((cols[:M], -cols[M:]), axis=0)

    vals = jnp.concatenate(
        (residual, (trace_cell + 1).astype(F32)[None, :], jnp.zeros((7, points), F32)), axis=0
    )
    packed = pack_points(trace_dest, vals, tiles, cap)
    packed = packed.reshape(own + 8, tiles, cap).transpose(1, 0, 2)
    got = lax.all_to_all(packed, ("row", "col"), split_axis=0, concat_axis=0, tiled=True)
    got = got.transpose(1, 0, 2).reshape(own + 8, tiles * cap)
    cell = got[own].astype(jnp.int32) - 1
    rowid = jnp.where(cell < 0, -1, cell // width)[None, :]
    colid = jnp.where(cell < 0, -1, cell % width)[:, None]

    part = field_modes(field, ch.reshape(1), own, cols_t, rows, forward_scale)
    spec = device_sum(part.reshape(-1), n_row, n_col, 0).reshape(inputs, 2, MODES)
    spec_re, spec_im = spec[:, 0], spec[:, 1]

    allowed = mode_mask(kept_modes)
    own_allowed = lax.dynamic_slice_in_dim(allowed, first, own, 0)
    out_w = lax.dynamic_slice_in_dim(spec_weight, first, own, 2)
    mixed_re = own_allowed * jnp.sum(
        out_w[0] * spec_re[:, None, :] - out_w[1] * spec_im[:, None, :], axis=0
    )
    mixed_im = own_allowed * jnp.sum(
        out_w[0] * spec_im[:, None, :] + out_w[1] * spec_re[:, None, :], axis=0
    )
    kron = spread_rows(lax.dynamic_slice_in_dim(point_weight, first, own, 1).T)
    slope, grad_part, point_part = slope_pass(
        field, mode_grid(mixed_re * mix_scale, mixed_im * mix_scale), wide_cols, cols_t, rows,
        rows_t, kron, jnp.repeat(bias, RB)[:, None], got[:own], rowid, colid, mix_scale,
    )
    swap = [(0, 1), (1, 0)]
    other_slope = lax.ppermute(slope, "ch", swap)

    summed = device_sum(
        jnp.concatenate((grad_part.reshape(-1), point_part.reshape(-1))), n_row, n_col, 1
    )
    mode_size = own * 2 * MODES
    modes = summed[:, :mode_size].reshape(inputs, 2, MODES)
    modes_re, modes_im = modes[:, 0], modes[:, 1]
    mine = lax.dynamic_slice_in_dim(summed, ch, 1, 0)[0]
    own_modes = mine[:mode_size].reshape(own, 2, MODES)
    own_gre, own_gim = own_modes[:, 0], own_modes[:, 1]
    norm_points = 1.0 / math.sqrt(points_all)
    grad_point = mine[mode_size:].reshape(inputs, own) * norm_points
    grad_bias = own_gre[:, 0] * (norm_points / mix_scale)

    grad_scale = math.sqrt(MODES / points_all)
    keep_re = own_allowed * own_gre * grad_scale
    keep_im = own_allowed * own_gim * grad_scale
    grad_spec = jnp.stack(
        (
            keep_re[None] * spec_re[:, None] + keep_im[None] * spec_im[:, None],
            keep_im[None] * spec_re[:, None] - keep_re[None] * spec_im[:, None],
        ),
        axis=0,
    )
    in_w = lax.dynamic_slice_in_dim(spec_weight, first, own, 1)
    all_re = allowed * modes_re * forward_scale
    all_im = allowed * modes_im * forward_scale
    adjoint_re = jnp.sum(in_w[0] * all_re[None] + in_w[1] * all_im[None], axis=1)
    adjoint_im = jnp.sum(in_w[0] * all_im[None] - in_w[1] * all_re[None], axis=1)
    own_point = lax.dynamic_slice_in_dim(point_weight, first, own, 0)
    kron_own = spread_rows(lax.dynamic_slice_in_dim(own_point, first, own, 1))
    kron_other = spread_rows(lax.dynamic_slice_in_dim(own_point, own - first, own, 1))
    grad_field = back_pass(
        slope, other_slope, mode_grid(adjoint_re, adjoint_im), rows_t, wide_cols, kron_own,
        kron_other,
    )
    return (grad_field, grad_spec, grad_point, grad_bias)


def solution(mesh):
    return jax.shard_map(
        per_device,
        mesh=mesh,
        in_specs=(
            P(None, "row", "col"),
            P(),
            P(),
            P("ch"),
            P(),
            P("ch", ("row", "col")),
            P(("row", "col"), None),
            P(("row", "col")),
        ),
        out_specs=(P("ch", "row", "col"), P(None, None, "ch", None), P(None, "ch"), P("ch")),
        check_vma=False,
    )
```

```python
import functools
import math

import jax
import jax.numpy as jnp
from jax import lax
from jax.experimental import pallas as pl
from jax.experimental.pallas import tpu as pltpu
from jax.sharding import PartitionSpec as P

M = 16
A = 2 * M
MODES = A * M
RB = 8
F32 = jnp.float32
BF16 = jnp.bfloat16
FULL_TURN = 6.283185307179586
NN = (((1,), (0,)), ((), ()))
NT = (((1,), (1,)), ((), ()))
MIB = 1 << 20


def row_table(start_at, extent, period):
    frequency = jnp.arange(A, dtype=jnp.int32)
    frequency = jnp.where(frequency < M, frequency, frequency - A)
    places = start_at + jnp.arange(extent, dtype=jnp.int32)
    phases = frequency[:, None] * places[None, :] % period
    angles = phases.astype(F32) * (FULL_TURN / period)
    return jnp.concatenate((jnp.cos(angles), jnp.sin(angles)), axis=0)


def col_table(start_at, extent, period):
    frequency = jnp.arange(M, dtype=jnp.int32)
    places = start_at + jnp.arange(extent, dtype=jnp.int32)
    phases = frequency[:, None] * places[None, :] % period
    angles = phases.astype(F32) * (FULL_TURN / period)
    return jnp.concatenate((jnp.cos(angles), jnp.sin(angles)), axis=0)


def mode_mask(kept_modes):
    indices = jnp.arange(MODES, dtype=jnp.int32)
    row_mode = indices // M
    col_mode = indices % M
    row_rank = jnp.where(row_mode < M, row_mode, 2 * M - 1 - row_mode)
    allowed = (row_rank[None, :] < kept_modes[:, None]) & (col_mode[None, :] < kept_modes[:, None])
    return allowed.astype(F32)


def split2(x):
    hi = x.astype(BF16)
    return hi, (x - hi.astype(F32)).astype(BF16)


def mm(a, b, dims=NN):
    return lax.dot_general(a, b, dims, preferred_element_type=F32)


def dot3(a, b, dims=NN):
    return mm(a[0], b[0], dims) + (mm(a[0], b[1], dims) + mm(a[1], b[0], dims))


def stacked(x, axis):
    hi, low = split2(x)
    return jnp.concatenate((hi.astype(F32), low.astype(F32)), axis=axis).astype(BF16)


def dot_tall(a_stack, b):
    count = a_stack.shape[0] // 2
    hi, low = split2(b)
    both = mm(a_stack, hi)
    return both[:count] + both[count:] + mm(a_stack[:count], low)


def deep_left(x):
    hi = x.astype(BF16).astype(F32)
    return jnp.concatenate((hi, x - hi, hi), axis=1)


def deep_right(x):
    hi = x.astype(BF16).astype(F32)
    return jnp.concatenate((hi, hi, x - hi), axis=0).astype(BF16)


def pack(dest, vals, out_ref, tiles, cap):
    n = dest.shape[0]
    wide = max(tiles, 128)
    named = dest == lax.broadcasted_iota(jnp.int32, (n, wide), 1)
    one_hot = named.astype(F32).astype(BF16)
    before = (
        lax.broadcasted_iota(jnp.int32, (n, n), 1) < lax.broadcasted_iota(jnp.int32, (n, n), 0)
    )
    earlier = mm(before.astype(F32).astype(BF16), one_hot)
    rank = jnp.sum(jnp.where(named, earlier, 0.0), axis=1, keepdims=True)
    position = dest * cap + rank.astype(jnp.int32)
    rows = vals.shape[0]
    hi = vals.astype(BF16)
    left = vals - hi.astype(F32)
    mid = left.astype(BF16)
    low = (left - mid.astype(F32)).astype(BF16)
    parts = jnp.concatenate((hi.astype(F32), mid.astype(F32), low.astype(F32)), axis=0).astype(BF16)
    step = 512
    for first in range(0, tiles * cap, step):
        at = lax.broadcasted_iota(jnp.int32, (n, step), 1) + first
        place = (position == at).astype(F32).astype(BF16)
        got = mm(parts, place)
        got = got[:rows] + got[rows : 2 * rows] + got[2 * rows : 3 * rows]
        for at in range(0, step, cap):
            out_ref[(first + at) // cap] = got[:, at : at + cap]


def to_modes(rows_stack, tall, out_ref, at, scale):
    both = mm(rows_stack, stacked(tall, 1))
    grid = both[: 2 * A, : 2 * M] + both[2 * A :, : 2 * M] + both[: 2 * A, 2 * M :]
    out_ref[at, 0] = (grid[:A, :M] - grid[A:, M:]) * scale
    out_ref[at, 1] = (grid[A:, :M] + grid[:A, M:]) * (-scale)


def slope_kernel(
    scale, field_ref, grid_ref, tall_rows_ref, wide_cols_ref, tall_cols_ref, rows_ref, kron_ref,
    bias_ref, vals_ref, rowid_ref, colid_ref, group_ref,
    slope_ref, modes_ref, point_ref,
    half_ref, hot_ref, v_ref, tall_ref, acc_ref, kron2_ref, wide2_ref, cols2_ref,
):
    step = pl.program_id(0)
    channels, block, width = slope_ref.shape
    rows = channels * RB
    points = vals_ref.shape[1]
    inputs = field_ref.shape[0]

    @pl.when(step == 0)
    def _():
        tall_rows = deep_left(tall_rows_ref[...]).astype(BF16)
        for o in range(channels):
            half_ref[o] = deep_left(mm(tall_rows, deep_right(grid_ref[o])))
        vals = vals_ref[...]
        hi = vals.astype(BF16).astype(F32)
        both = jnp.concatenate((hi, vals - hi), axis=0)
        both = jnp.broadcast_to(both[:, None, :], (2 * channels, RB, points))
        v_ref[...] = both.reshape(2 * rows, points).astype(BF16)
        part = 256
        for first in range(0, points, part):
            ids = colid_ref[first : first + part, :]
            hot = ids == lax.broadcasted_iota(jnp.int32, (part, width), 1)
            hot_ref[first : first + part, :] = hot.astype(F32).astype(BF16)
        acc_ref[...] = jnp.zeros_like(acc_ref)
        kron2_ref[...] = stacked(kron_ref[...], 0)
        wide2_ref[...] = deep_right(wide_cols_ref[...])
        cols2_ref[...] = stacked(tall_cols_ref[...], 1)

    subs = block // RB
    picked = []
    for u in range(subs):
        first = step * block + u * RB
        here = rowid_ref[...] == first + lax.broadcasted_iota(jnp.int32, (RB, points), 0)
        here = here.astype(F32)
        here = jnp.concatenate((here, here), axis=0).astype(BF16)
        here = jnp.broadcast_to(here[None], (rows // RB, 2 * RB, points)).reshape(2 * rows, points)
        picked.append(v_ref[...] * here)
    cots = mm(jnp.concatenate(picked, axis=0), hot_ref[...])
    k = math.sqrt(2.0 / math.pi)
    fields, slopes = [], []
    for u in range(subs):
        first = pl.multiple_of(step * block + u * RB, RB)
        hi, low = split2(field_ref[:, u * RB : (u + 1) * RB, :].reshape(inputs * RB, width))
        half = half_ref[:, pl.ds(first, RB), :].reshape(rows, 6 * M).astype(BF16)
        both = mm(kron2_ref[...], hi)
        pre = (
            mm(half, wide2_ref[...])
            + (both[:rows] + both[rows:] + mm(kron2_ref[:rows, :], low))
            + bias_ref[...]
        )
        cot = cots[2 * rows * u : 2 * rows * u + rows] + cots[2 * rows * u + rows : 2 * rows * (u + 1)]
        square = pre * pre
        t = jnp.tanh(k * pre * (1.0 + 0.044715 * square))
        rate = 0.5 * (1.0 + t) + 0.5 * k * pre * (1.0 - t * t) * (1.0 + 3 * 0.044715 * square)
        slope = cot * rate
        slope_ref[:, u * RB : (u + 1) * RB, :] = slope.reshape(channels, RB, width)
        parts = stacked(slope, 0)
        got = mm(parts, cols2_ref[...])
        tall = got[:rows, : 2 * M] + got[:rows, 2 * M :] + got[rows:, : 2 * M]
        tall_ref[:, pl.ds(first, RB), :] = tall.reshape(channels, RB, 2 * M)
        fields.append(jnp.concatenate((hi, low), axis=0))
        slopes.append(parts)
    acc_ref[...] += mm(jnp.concatenate(fields, axis=1), jnp.concatenate(slopes, axis=1), NT)

    @pl.when(step == pl.num_programs(0) - 1)
    def _():
        rows_stack = stacked(rows_ref[...], 0)
        for o in range(channels):
            to_modes(rows_stack, tall_ref[o], modes_ref, o, scale)
        total = acc_ref[: inputs * RB, :] + acc_ref[inputs * RB :, :]
        total = total[:, :rows] + total[:, rows:]
        same = lax.broadcasted_iota(jnp.int32, total.shape, 0) % RB == (
            lax.broadcasted_iota(jnp.int32, total.shape, 1) % RB
        )
        kept = jnp.sum(jnp.where(same, total, 0.0).reshape(inputs, RB, rows), axis=1)
        point_ref[...] = lax.dot_general(
            kept, group_ref[...], NN, precision=lax.Precision.HIGHEST, preferred_element_type=F32
        )


def whole(shape):
    return pl.BlockSpec(shape, lambda i: (0,) * len(shape))


def slope_pass(field, grid, wide_cols, cols_t, rows, rows_t, kron, bias, vals, rowid, colid, scale):
    inputs, height, width = field.shape
    channels = grid.shape[0]
    points = vals.shape[1]
    lanes = channels * RB
    group = (
        jnp.arange(lanes, dtype=jnp.int32)[:, None] // RB
        == jnp.arange(channels, dtype=jnp.int32)[None, :]
    ).astype(F32)
    args = (field, grid, rows_t, wide_cols, cols_t, rows, kron, bias, vals, rowid, colid, group)
    return pl.pallas_call(
        functools.partial(slope_kernel, scale),
        grid=(height // (2 * RB),),
        in_specs=[pl.BlockSpec((inputs, 2 * RB, width), lambda i: (0, i, 0))]
        + [whole(arg.shape) for arg in args[1:]],
        out_specs=[
            pl.BlockSpec((channels, 2 * RB, width), lambda i: (0, i, 0)),
            whole((channels, 2, A, M)),
            whole((inputs, channels)),
        ],
        out_shape=[
            jax.ShapeDtypeStruct((channels, height, width), F32),
            jax.ShapeDtypeStruct((channels, 2, A, M), F32),
            jax.ShapeDtypeStruct((inputs, channels), F32),
        ],
        scratch_shapes=[
            pltpu.VMEM((channels, height, 6 * M), F32),
            pltpu.VMEM((points, width), BF16),
            pltpu.VMEM((2 * lanes, points), BF16),
            pltpu.VMEM((channels, height, 2 * M), F32),
            pltpu.VMEM((2 * inputs * RB, 2 * lanes), F32),
            pltpu.VMEM((2 * lanes, inputs * RB), BF16),
            pltpu.VMEM((6 * M, width), BF16),
            pltpu.VMEM((width, 4 * M), BF16),
        ],
        compiler_params=pltpu.CompilerParams(vmem_limit_bytes=52 * MIB),
    )(*args)


def back_kernel(
    own_ref, other_ref, grid_ref, tall_rows_ref, wide_cols_ref, kron_ref, out_ref,
    half_ref, kron2_ref, wide2_ref,
):
    step = pl.program_id(0)
    channels, block, width = out_ref.shape
    rows = channels * RB

    @pl.when(step == 0)
    def _():
        tall_rows = deep_left(tall_rows_ref[...]).astype(BF16)
        for c in range(channels):
            half_ref[c] = deep_left(mm(tall_rows, deep_right(grid_ref[c])))
        kron2_ref[...] = stacked(kron_ref[...], 0)
        wide2_ref[...] = deep_right(wide_cols_ref[...])

    for u in range(block // RB):
        at = slice(u * RB, (u + 1) * RB)
        first = pl.multiple_of(step * block + u * RB, RB)
        half = half_ref[:, pl.ds(first, RB), :].reshape(rows, 6 * M).astype(BF16)
        slope = jnp.concatenate(
            (own_ref[:, at, :].reshape(rows, width), other_ref[:, at, :].reshape(rows, width)),
            axis=0,
        )
        result = mm(half, wide2_ref[...]) + dot_tall(kron2_ref[...], slope)
        out_ref[:, at, :] = result.reshape(channels, RB, width)


def back_pass(own, other, grid, rows_t, wide_cols, kron):
    channels, height, width = own.shape
    args = (own, other, grid, rows_t, wide_cols, kron)
    block = pl.BlockSpec((channels, 4 * RB, width), lambda i: (0, i, 0))
    return pl.pallas_call(
        back_kernel,
        grid=(height // (4 * RB),),
        in_specs=[block, block] + [whole(arg.shape) for arg in args[2:]],
        out_specs=block,
        out_shape=jax.ShapeDtypeStruct((channels, height, width), F32),
        scratch_shapes=[
            pltpu.VMEM((channels, height, 6 * M), F32),
            pltpu.VMEM((2 * kron.shape[0], kron.shape[1]), BF16),
            pltpu.VMEM((6 * M, width), BF16),
        ],
        compiler_params=pltpu.CompilerParams(vmem_limit_bytes=40 * MIB),
    )(*args)


MESH = pl.DeviceIdType.MESH


def greet_all(n_row, n_col):
    n = n_row * n_col
    barrier = pltpu.get_barrier_semaphore()

    def greet(i, carry):
        pl.semaphore_signal(
            barrier, inc=1, device_id=device_at(n_row, n_col, i // 2, i % 2), device_id_type=MESH
        )
        return carry

    lax.fori_loop(1, 2 * n, greet, 0)
    return barrier


def device_at(n_row, n_col, offset, flip):
    n = n_row * n_col
    at = lax.rem(lax.axis_index("row") * n_col + lax.axis_index("col") + offset, n)
    return (at // n_col, lax.rem(at, n_col), lax.rem(lax.axis_index("ch") + flip, 2))


def send_slices(n_row, n_col, x_ref, landed, send, recv):
    n = n_row * n_col
    me = lax.axis_index("row") * n_col + lax.axis_index("col")

    def copy(k):
        return pltpu.make_async_remote_copy(
            src_ref=x_ref.at[lax.rem(me + k, n)],
            dst_ref=landed.at[k],
            send_sem=send.at[k],
            recv_sem=recv.at[k],
            device_id=device_at(n_row, n_col, k, 0),
            device_id_type=MESH,
        )

    def start(k, carry):
        copy(k).start()
        return carry

    lax.fori_loop(1, n, start, 0)
    return copy


def sum_all(n_row, n_col, x_ref, landed, total, gathered, send1, recv1, send2, recv2):
    n = n_row * n_col
    ch = lax.axis_index("ch")
    me = lax.axis_index("row") * n_col + lax.axis_index("col")
    scatter = send_slices(n_row, n_col, x_ref, landed, send1, recv1)
    total[...] = x_ref[me]

    def take(k, carry):
        scatter(k).wait_recv()
        total[...] += landed[k]
        return carry

    lax.fori_loop(1, n, take, 0)
    gathered[ch * n + me] = total[...]

    def spread(i):
        return pltpu.make_async_remote_copy(
            src_ref=total,
            dst_ref=gathered.at[ch * n + me],
            send_sem=send2.at[i],
            recv_sem=recv2.at[i],
            device_id=device_at(n_row, n_col, i // 2, i % 2),
            device_id_type=MESH,
        )

    def start2(i, carry):
        spread(i).start()
        return carry

    lax.fori_loop(1, 2 * n, start2, 0)

    def end1(k, carry):
        scatter(k).wait_send()
        return carry

    lax.fori_loop(1, n, end1, 0)

    def end2(i, carry):
        spread(i).wait()
        return carry

    lax.fori_loop(1, 2 * n, end2, 0)


def sum_kernel(n_row, n_col, x_ref, out_ref, landed, total, gathered, send1, recv1, send2, recv2):
    barrier = greet_all(n_row, n_col)
    pl.semaphore_wait(barrier, 2 * n_row * n_col - 1)
    sum_all(n_row, n_col, x_ref, landed, total, gathered, send1, recv1, send2, recv2)
    out_ref[...] = gathered[...]


def front_kernel(
    n_row, n_col, own, scale, dest_ref, vals_ref, cols_ref, rows_ref, field_ref, got_ref, out_ref,
    held, held_sem, grouped, came, tall_ref, x_ref, landed, total, gathered,
    send0, recv0, send1, recv1, send2, recv2,
):
    n = n_row * n_col
    count, height, width = held.shape[1:]
    cap = grouped.shape[2]
    ch = lax.axis_index("ch")
    me = lax.axis_index("row") * n_col + lax.axis_index("col")
    loads = [
        pltpu.make_async_copy(
            field_ref.at[pl.ds(ch * own + i * count, count)], held.at[i], held_sem.at[i]
        )
        for i in range(own // count)
    ]
    for load in loads:
        load.start()
    barrier = greet_all(n_row, n_col)
    pack(dest_ref[...], vals_ref[...], grouped, n, cap)
    pl.semaphore_wait(barrier, 2 * n - 1)
    trade = send_slices(n_row, n_col, grouped, came, send0, recv0)
    came[0] = grouped[me]

    cols2 = stacked(cols_ref[...], 1)
    for i, load in enumerate(loads):
        load.wait()
        both = mm(stacked(held[i].reshape(count * height, width), 0), cols2)
        half = count * height
        tall = both[:half, : 2 * M] + both[:half, 2 * M :] + both[half:, : 2 * M]
        for c in range(count):
            at = (i * count + c) * M
            tall_ref[:, at : at + M] = tall[c * height : (c + 1) * height, :M]
            at = at + own * M
            tall_ref[:, at : at + M] = tall[c * height : (c + 1) * height, M:]
    side = own * M
    both = mm(stacked(rows_ref[...], 0), stacked(tall_ref[...], 1))
    grid = both[: 2 * A, : 2 * side] + both[2 * A :, : 2 * side] + both[: 2 * A, 2 * side :]
    re = (grid[:A, :side] - grid[A:, side:]) * scale
    im = (grid[A:, :side] + grid[:A, side:]) * (-scale)
    lines = jnp.concatenate(
        [part[:, at : at + 128] for part in (re, im) for at in range(0, side, 128)], axis=0
    )
    deep = lines.shape[0] // n
    for p in range(n):
        x_ref[p] = lines[p * deep : (p + 1) * deep]
    sum_all(n_row, n_col, x_ref, landed, total, gathered, send1, recv1, send2, recv2)
    out_ref[...] = gathered[...]

    def end0(k, carry):
        trade(k).wait()
        return carry

    lax.fori_loop(1, n, end0, 0)
    for p in range(n):
        got_ref[:, p * cap : (p + 1) * cap] = came[p]


def front_pass(dest, vals, cols_t, rows, field, own, cap, scale, n_row, n_col):
    n = n_row * n_col
    _, height, width = field.shape
    count = 4
    deep = own * 2 * MODES // 128 // n
    kept = vals.shape[0]
    vmem = pl.BlockSpec(memory_space=pltpu.VMEM)
    got, out = pl.pallas_call(
        functools.partial(front_kernel, n_row, n_col, own, scale),
        out_shape=[
            jax.ShapeDtypeStruct((kept, n * cap), F32),
            jax.ShapeDtypeStruct((2 * n, deep, 128), F32),
        ],
        in_specs=[vmem, vmem, vmem, vmem, pl.BlockSpec(memory_space=pl.ANY)],
        out_specs=[vmem, vmem],
        scratch_shapes=[
            pltpu.VMEM((own // count, count, height, width), F32),
            pltpu.SemaphoreType.DMA((own // count,)),
            pltpu.VMEM((n, kept, cap), F32),
            pltpu.VMEM((n, kept, cap), F32),
            pltpu.VMEM((height, 2 * own * M), F32),
            pltpu.VMEM((n, deep, 128), F32),
            pltpu.VMEM((n, deep, 128), F32),
            pltpu.VMEM((deep, 128), F32),
            pltpu.VMEM((2 * n, deep, 128), F32),
        ]
        + [pltpu.SemaphoreType.DMA((n,))] * 4
        + [pltpu.SemaphoreType.DMA((2 * n,))] * 2,
        compiler_params=pltpu.CompilerParams(
            collective_id=0, has_side_effects=True, vmem_limit_bytes=44 * MIB
        ),
    )(dest, vals, cols_t, rows, field)
    wide = 128 // M
    spec = out.reshape(2, 2, own // wide, A, wide, M).transpose(1, 0, 2, 4, 3, 5)
    return got, spec.reshape(2, 2 * own, MODES)


def device_sum(x, n_row, n_col, which):
    n = n_row * n_col
    size = x.shape[0]
    tall = -(-size // (n * 128))
    x = jnp.pad(x, (0, n * tall * 128 - size)).reshape(n, tall, 128)
    out = pl.pallas_call(
        functools.partial(sum_kernel, n_row, n_col),
        out_shape=jax.ShapeDtypeStruct((2 * n, tall, 128), F32),
        in_specs=[pl.BlockSpec(memory_space=pltpu.VMEM)],
        out_specs=pl.BlockSpec(memory_space=pltpu.VMEM),
        scratch_shapes=[
            pltpu.VMEM((n, tall, 128), F32),
            pltpu.VMEM((tall, 128), F32),
            pltpu.VMEM((2 * n, tall, 128), F32),
            pltpu.SemaphoreType.DMA((n,)),
            pltpu.SemaphoreType.DMA((n,)),
            pltpu.SemaphoreType.DMA((2 * n,)),
            pltpu.SemaphoreType.DMA((2 * n,)),
        ],
        compiler_params=pltpu.CompilerParams(collective_id=which, has_side_effects=True),
    )(x)
    return out.reshape(2, n * tall * 128)[:, :size]


def mode_grid(re, im):
    count = re.shape[0]
    re = re.reshape(count, A, M)
    im = im.reshape(count, A, M)
    return jnp.concatenate(
        (jnp.concatenate((re, im), axis=2), jnp.concatenate((-im, re), axis=2)), axis=1
    )


def spread_rows(weights):
    eye = jnp.eye(RB, dtype=F32)
    a, b = weights.shape
    return (weights[:, None, :, None] * eye[None, :, None, :]).reshape(a * RB, b * RB)


def per_device(
    field, spec_weight, point_weight, bias, kept_modes, residual, trace_dest, trace_cell
):
    n_row = lax.axis_size("row")
    n_col = lax.axis_size("col")
    ch = lax.axis_index("ch")
    inputs, height, width = field.shape
    own = inputs // lax.axis_size("ch")
    first = ch * own
    points = trace_dest.shape[0]
    tiles = n_row * n_col
    points_all = points * tiles
    cap = max(2, 2 * points // tiles)
    forward_scale = 1.0 / math.sqrt(height * n_row * width * n_col)
    mix_scale = 1.0 / math.sqrt(MODES)

    rows = row_table(lax.axis_index("row") * height, height, height * n_row)
    cols = col_table(lax.axis_index("col") * width, width, width * n_col)
    rows_t = rows.T
    cols_t = cols.T
    wide_cols = jnp.concatenate((cols[:M], -cols[M:]), axis=0)

    vals = jnp.concatenate(
        (residual, (trace_cell + 1).astype(F32)[None, :], jnp.zeros((7, points), F32)), axis=0
    )
    got, spec = front_pass(
        trace_dest, vals, cols_t, rows, field, own, cap, forward_scale, n_row, n_col
    )
    spec_re, spec_im = spec[0], spec[1]
    cell = got[own].astype(jnp.int32) - 1
    rowid = jnp.where(cell < 0, -1, cell // width)[None, :]
    colid = jnp.where(cell < 0, -1, cell % width)[:, None]

    allowed = mode_mask(kept_modes)
    own_allowed = lax.dynamic_slice_in_dim(allowed, first, own, 0)
    out_w = lax.dynamic_slice_in_dim(spec_weight, first, own, 2)
    mixed_re = own_allowed * jnp.sum(
        out_w[0] * spec_re[:, None, :] - out_w[1] * spec_im[:, None, :], axis=0
    )
    mixed_im = own_allowed * jnp.sum(
        out_w[0] * spec_im[:, None, :] + out_w[1] * spec_re[:, None, :], axis=0
    )
    kron = spread_rows(lax.dynamic_slice_in_dim(point_weight, first, own, 1).T)
    slope, grad_part, point_part = slope_pass(
        field, mode_grid(mixed_re * mix_scale, mixed_im * mix_scale), wide_cols, cols_t, rows,
        rows_t, kron, jnp.repeat(bias, RB)[:, None], got[:own], rowid, colid, mix_scale,
    )
    swap = [(0, 1), (1, 0)]
    other_slope = lax.ppermute(slope, "ch", swap)

    summed = device_sum(
        jnp.concatenate((grad_part.reshape(-1), point_part.reshape(-1))), n_row, n_col, 1
    )
    mode_size = own * 2 * MODES
    modes = summed[:, :mode_size].reshape(inputs, 2, MODES)
    modes_re, modes_im = modes[:, 0], modes[:, 1]
    mine = lax.dynamic_slice_in_dim(summed, ch, 1, 0)[0]
    own_modes = mine[:mode_size].reshape(own, 2, MODES)
    own_gre, own_gim = own_modes[:, 0], own_modes[:, 1]
    norm_points = 1.0 / math.sqrt(points_all)
    grad_point = mine[mode_size:].reshape(inputs, own) * norm_points
    grad_bias = own_gre[:, 0] * (norm_points / mix_scale)

    grad_scale = math.sqrt(MODES / points_all)
    keep_re = own_allowed * own_gre * grad_scale
    keep_im = own_allowed * own_gim * grad_scale
    grad_spec = jnp.stack(
        (
            keep_re[None] * spec_re[:, None] + keep_im[None] * spec_im[:, None],
            keep_im[None] * spec_re[:, None] - keep_re[None] * spec_im[:, None],
        ),
        axis=0,
    )
    in_w = lax.dynamic_slice_in_dim(spec_weight, first, own, 1)
    all_re = allowed * modes_re * forward_scale
    all_im = allowed * modes_im * forward_scale
    adjoint_re = jnp.sum(in_w[0] * all_re[None] + in_w[1] * all_im[None], axis=1)
    adjoint_im = jnp.sum(in_w[0] * all_im[None] - in_w[1] * all_re[None], axis=1)
    own_point = lax.dynamic_slice_in_dim(point_weight, first, own, 0)
    kron_back = spread_rows(
        jnp.concatenate(
            (
                lax.dynamic_slice_in_dim(own_point, first, own, 1),
                lax.dynamic_slice_in_dim(own_point, own - first, own, 1),
            ),
            axis=1,
        )
    )
    grad_field = back_pass(
        slope, other_slope, mode_grid(adjoint_re, adjoint_im), rows_t, wide_cols, kron_back
    )
    return (grad_field, grad_spec, grad_point, grad_bias)


def solution(mesh):
    return jax.shard_map(
        per_device,
        mesh=mesh,
        in_specs=(
            P(None, "row", "col"),
            P(),
            P(),
            P("ch"),
            P(),
            P("ch", ("row", "col")),
            P(("row", "col"), None),
            P(("row", "col")),
        ),
        out_specs=(P("ch", "row", "col"), P(None, None, "ch", None), P(None, "ch"), P("ch")),
        check_vma=False,
    )
```

```python
import functools
import math

import jax
import jax.numpy as jnp
from jax import lax
from jax.experimental import pallas as pl
from jax.experimental.pallas import tpu as pltpu
from jax.sharding import PartitionSpec as P

M = 16
A = 2 * M
MODES = A * M
RB = 8
F32 = jnp.float32
BF16 = jnp.bfloat16
FULL_TURN = 6.283185307179586
NN = (((1,), (0,)), ((), ()))
NT = (((1,), (1,)), ((), ()))
MIB = 1 << 20


def row_table(start_at, extent, period):
    frequency = jnp.arange(A, dtype=jnp.int32)
    frequency = jnp.where(frequency < M, frequency, frequency - A)
    places = start_at + jnp.arange(extent, dtype=jnp.int32)
    phases = frequency[:, None] * places[None, :] % period
    angles = phases.astype(F32) * (FULL_TURN / period)
    return jnp.concatenate((jnp.cos(angles), jnp.sin(angles)), axis=0)


def col_table(start_at, extent, period):
    frequency = jnp.arange(M, dtype=jnp.int32)
    places = start_at + jnp.arange(extent, dtype=jnp.int32)
    phases = frequency[:, None] * places[None, :] % period
    angles = phases.astype(F32) * (FULL_TURN / period)
    return jnp.concatenate((jnp.cos(angles), jnp.sin(angles)), axis=0)


def mode_mask(kept_modes):
    indices = jnp.arange(MODES, dtype=jnp.int32)
    row_mode = indices // M
    col_mode = indices % M
    row_rank = jnp.where(row_mode < M, row_mode, 2 * M - 1 - row_mode)
    allowed = (row_rank[None, :] < kept_modes[:, None]) & (col_mode[None, :] < kept_modes[:, None])
    return allowed.astype(F32)


def split2(x):
    hi = x.astype(BF16)
    return hi, (x - hi.astype(F32)).astype(BF16)


def mm(a, b, dims=NN):
    return lax.dot_general(a, b, dims, preferred_element_type=F32)


def dot3(a, b, dims=NN):
    return mm(a[0], b[0], dims) + (mm(a[0], b[1], dims) + mm(a[1], b[0], dims))


def stacked(x, axis):
    hi, low = split2(x)
    return jnp.concatenate((hi.astype(F32), low.astype(F32)), axis=axis).astype(BF16)


def dot_tall(a_stack, b):
    count = a_stack.shape[0] // 2
    hi, low = split2(b)
    both = mm(a_stack, hi)
    return both[:count] + both[count:] + mm(a_stack[:count], low)


def deep_left(x):
    hi = x.astype(BF16).astype(F32)
    return jnp.concatenate((hi, x - hi, hi), axis=1)


def deep_right(x):
    hi = x.astype(BF16).astype(F32)
    return jnp.concatenate((hi, hi, x - hi), axis=0).astype(BF16)


def pack(dest, vals, out_ref, tiles, cap):
    n = dest.shape[0]
    wide = max(tiles, 128)
    named = dest == lax.broadcasted_iota(jnp.int32, (n, wide), 1)
    one_hot = named.astype(F32).astype(BF16)
    before = (
        lax.broadcasted_iota(jnp.int32, (n, n), 1) < lax.broadcasted_iota(jnp.int32, (n, n), 0)
    )
    earlier = mm(before.astype(F32).astype(BF16), one_hot)
    rank = jnp.sum(jnp.where(named, earlier, 0.0), axis=1, keepdims=True)
    position = dest * cap + rank.astype(jnp.int32)
    rows = vals.shape[0]
    hi = vals.astype(BF16)
    left = vals - hi.astype(F32)
    mid = left.astype(BF16)
    low = (left - mid.astype(F32)).astype(BF16)
    parts = jnp.concatenate((hi.astype(F32), mid.astype(F32), low.astype(F32)), axis=0).astype(BF16)
    step = 512
    for first in range(0, tiles * cap, step):
        at = lax.broadcasted_iota(jnp.int32, (n, step), 1) + first
        place = (position == at).astype(F32).astype(BF16)
        got = mm(parts, place)
        got = got[:rows] + got[rows : 2 * rows] + got[2 * rows : 3 * rows]
        for at in range(0, step, cap):
            out_ref[(first + at) // cap] = got[:, at : at + cap]


def mode_lines(rows, tall, scale):
    side = tall.shape[1] // 2
    both = mm(stacked(rows, 0), stacked(tall, 1))
    grid = both[: 2 * A, : 2 * side] + both[2 * A :, : 2 * side] + both[: 2 * A, 2 * side :]
    re = (grid[:A, :side] - grid[A:, side:]) * scale
    im = (grid[A:, :side] + grid[:A, side:]) * (-scale)
    return [part[:, at : at + 128] for part in (re, im) for at in range(0, side, 128)]


def exact(a, b):
    return lax.dot_general(
        a, b, NN, precision=lax.Precision.HIGHEST, preferred_element_type=F32
    )


def iota(shape, axis):
    return lax.broadcasted_iota(jnp.int32, shape, axis)


def spread_rows(weights):
    a, b = weights.shape
    left = (iota((a * RB, a), 0) // RB == iota((a * RB, a), 1)).astype(F32)
    right = (iota((b, b * RB), 1) // RB == iota((b, b * RB), 0)).astype(F32)
    shape = (a * RB, b * RB)
    same = iota(shape, 0) % RB == iota(shape, 1) % RB
    return jnp.where(same, exact(exact(left, weights), right), 0.0)


def slope_kernel(
    n_row, n_col, scale, field_ref, grid_ref, tall_rows_ref, wide_cols_ref, tall_cols_ref,
    rows_ref, point_ref, bias_ref, got_ref,
    slope_ref, other_ref, out_ref,
    half_ref, hot_ref, v_ref, tall_ref, acc_ref, kron2_ref, wide2_ref, cols2_ref, rowid_ref,
    made_ref, swap_send, swap_recv, x_ref, landed, total, gathered, send1, recv1, send2, recv2,
):
    step = pl.program_id(0)
    n = n_row * n_col
    channels, block, width = slope_ref.shape
    steps = made_ref.shape[0]
    rows = channels * RB
    points = got_ref.shape[1]
    inputs = field_ref.shape[0]

    def swap(i):
        return pltpu.make_async_remote_copy(
            src_ref=made_ref.at[i],
            dst_ref=other_ref.at[:, pl.ds(i * block, block), :],
            send_sem=swap_send.at[i],
            recv_sem=swap_recv.at[i],
            device_id=device_at(n_row, n_col, 0, 1),
            device_id_type=MESH,
        )

    @pl.when(step == 0)
    def _():
        greet_all(n_row, n_col)
        tall_rows = deep_left(tall_rows_ref[...]).astype(BF16)
        for o in range(channels):
            half_ref[o] = deep_left(mm(tall_rows, deep_right(grid_ref[o])))
        vals = got_ref[:channels, :]
        hi = vals.astype(BF16).astype(F32)
        both = jnp.concatenate((hi, vals - hi), axis=0)
        both = jnp.broadcast_to(both[:, None, :], (2 * channels, RB, points))
        v_ref[...] = both.reshape(2 * rows, points).astype(BF16)
        cell = got_ref[channels : channels + 1, :].astype(jnp.int32) - 1
        rowid_ref[...] = jnp.where(cell < 0, -1, cell // width)
        colid = jnp.where(cell < 0, -1, cell % width).astype(F32)
        for first in range(0, points, 128):
            ids = jnp.broadcast_to(colid[:, first : first + 128], (128, 128)).T
            for at in range(0, width, 128):
                hot = ids == (iota((128, 128), 1) + at).astype(F32)
                hot_ref[first : first + 128, at : at + 128] = hot.astype(F32).astype(BF16)
        acc_ref[...] = jnp.zeros_like(acc_ref)
        kron2_ref[...] = stacked(spread_rows(point_ref[...]), 0)
        wide2_ref[...] = deep_right(wide_cols_ref[...])
        cols2_ref[...] = stacked(tall_cols_ref[...], 1)

    subs = block // RB
    picked = []
    for u in range(subs):
        first = step * block + u * RB
        here = rowid_ref[...] == first + lax.broadcasted_iota(jnp.int32, (RB, points), 0)
        here = here.astype(F32)
        here = jnp.concatenate((here, here), axis=0).astype(BF16)
        here = jnp.broadcast_to(here[None], (rows // RB, 2 * RB, points)).reshape(2 * rows, points)
        picked.append(v_ref[...] * here)
    cots = mm(jnp.concatenate(picked, axis=0), hot_ref[...])
    k = math.sqrt(2.0 / math.pi)
    fields, slopes = [], []
    for u in range(subs):
        first = pl.multiple_of(step * block + u * RB, RB)
        hi, low = split2(field_ref[:, u * RB : (u + 1) * RB, :].reshape(inputs * RB, width))
        half = half_ref[:, pl.ds(first, RB), :].reshape(rows, 6 * M).astype(BF16)
        both = mm(kron2_ref[...], hi)
        pre = (
            mm(half, wide2_ref[...])
            + (both[:rows] + both[rows:] + mm(kron2_ref[:rows, :], low))
            + bias_ref[...]
        )
        cot = cots[2 * rows * u : 2 * rows * u + rows] + cots[2 * rows * u + rows : 2 * rows * (u + 1)]
        square = pre * pre
        t = jnp.tanh(k * pre * (1.0 + 0.044715 * square))
        rate = 0.5 * (1.0 + t) + 0.5 * k * pre * (1.0 - t * t) * (1.0 + 3 * 0.044715 * square)
        slope = cot * rate
        slope_ref[:, u * RB : (u + 1) * RB, :] = slope.reshape(channels, RB, width)
        made_ref[step, :, u * RB : (u + 1) * RB, :] = slope.reshape(channels, RB, width)
        parts = stacked(slope, 0)
        got = mm(parts, cols2_ref[...])
        tall = got[:rows, : 2 * M] + got[:rows, 2 * M :] + got[rows:, : 2 * M]
        for o in range(channels):
            for part in range(2):
                at = (part * channels + o) * M
                tall_ref[pl.ds(first, RB), at : at + M] = tall[
                    o * RB : (o + 1) * RB, part * M : (part + 1) * M
                ]
        fields.append(jnp.concatenate((hi, low), axis=0))
        slopes.append(parts)
    acc_ref[...] += mm(jnp.concatenate(fields, axis=1), jnp.concatenate(slopes, axis=1), NT)

    @pl.when(step == 0)
    def _():
        pl.semaphore_wait(pltpu.get_barrier_semaphore(), 2 * n - 1)

    swap(step).start()

    @pl.when(step == steps - 1)
    def _():
        lines = mode_lines(rows_ref[...], tall_ref[...], scale)
        total_point = acc_ref[: inputs * RB, :] + acc_ref[inputs * RB :, :]
        total_point = total_point[:, :rows] + total_point[:, rows:]
        same = iota(total_point.shape, 0) % RB == iota(total_point.shape, 1) % RB
        kept = jnp.sum(jnp.where(same, total_point, 0.0).reshape(inputs, RB, rows), axis=1)
        each = 128 // channels
        group = (iota((rows, 128), 0) // RB == iota((rows, 128), 1) % channels).astype(F32)
        wide = exact(kept, group)
        own = iota(wide.shape, 1) // channels == iota(wide.shape, 0) % each
        lines.append(jnp.sum(jnp.where(own, wide, 0.0).reshape(inputs // each, each, 128), axis=1))
        deep = x_ref.shape[1]
        count = sum(line.shape[0] for line in lines)
        lines.append(jnp.zeros((n * deep - count, 128), F32))
        lines = jnp.concatenate(lines, axis=0)
        for p in range(n):
            x_ref[p] = lines[p * deep : (p + 1) * deep]
        sum_all(n_row, n_col, x_ref, landed, total, gathered, send1, recv1, send2, recv2)
        out_ref[...] = gathered[...]

        def end(i, carry):
            swap(i).wait()
            return carry

        lax.fori_loop(0, steps, end, 0)


def whole(shape):
    return pl.BlockSpec(shape, lambda i: (0,) * len(shape))


def slope_pass(
    field, grid, wide_cols, cols_t, rows, rows_t, point, bias, got, scale, n_row, n_col
):
    n = n_row * n_col
    inputs, height, width = field.shape
    channels = grid.shape[0]
    points = got.shape[1]
    lanes = channels * RB
    block = 2 * RB
    steps = height // block
    mode_count = channels * 2 * MODES // 128
    deep = -(-(mode_count + inputs * channels // 128) // n)
    args = (field, grid, rows_t, wide_cols, cols_t, rows, point, bias, got)
    slope, other, out = pl.pallas_call(
        functools.partial(slope_kernel, n_row, n_col, scale),
        grid=(steps,),
        in_specs=[pl.BlockSpec((inputs, block, width), lambda i: (0, i, 0))]
        + [whole(arg.shape) for arg in args[1:]],
        out_specs=[
            pl.BlockSpec((channels, block, width), lambda i: (0, i, 0)),
            pl.BlockSpec(memory_space=pl.ANY),
            whole((2 * n, deep, 128)),
        ],
        out_shape=[
            jax.ShapeDtypeStruct((channels, height, width), F32),
            jax.ShapeDtypeStruct((channels, height, width), F32),
            jax.ShapeDtypeStruct((2 * n, deep, 128), F32),
        ],
        scratch_shapes=[
            pltpu.VMEM((channels, height, 6 * M), F32),
            pltpu.VMEM((points, width), BF16),
            pltpu.VMEM((2 * lanes, points), BF16),
            pltpu.VMEM((height, 2 * channels * M), F32),
            pltpu.VMEM((2 * inputs * RB, 2 * lanes), F32),
            pltpu.VMEM((2 * lanes, inputs * RB), BF16),
            pltpu.VMEM((6 * M, width), BF16),
            pltpu.VMEM((width, 4 * M), BF16),
            pltpu.VMEM((1, points), jnp.int32),
            pltpu.VMEM((steps, channels, block, width), F32),
            pltpu.SemaphoreType.DMA((steps,)),
            pltpu.SemaphoreType.DMA((steps,)),
            pltpu.VMEM((n, deep, 128), F32),
            pltpu.VMEM((n, deep, 128), F32),
            pltpu.VMEM((deep, 128), F32),
            pltpu.VMEM((2 * n, deep, 128), F32),
            pltpu.SemaphoreType.DMA((n,)),
            pltpu.SemaphoreType.DMA((n,)),
            pltpu.SemaphoreType.DMA((2 * n,)),
            pltpu.SemaphoreType.DMA((2 * n,)),
        ],
        compiler_params=pltpu.CompilerParams(
            collective_id=1, has_side_effects=True, vmem_limit_bytes=54 * MIB
        ),
    )(*args)
    out = out.reshape(2, n * deep, 128)
    return slope, other, unfold(out[:, :mode_count], channels), out[:, mode_count:]


def back_kernel(
    own_ref, other_ref, grid_ref, tall_rows_ref, wide_cols_ref, point_ref, out_ref,
    half_ref, kron2_ref, wide2_ref,
):
    step = pl.program_id(0)
    channels, block, width = out_ref.shape
    rows = channels * RB

    @pl.when(step == 0)
    def _():
        tall_rows = deep_left(tall_rows_ref[...]).astype(BF16)
        for c in range(channels):
            half_ref[c] = deep_left(mm(tall_rows, deep_right(grid_ref[c])))
        kron2_ref[...] = stacked(spread_rows(point_ref[...]), 0)
        wide2_ref[...] = deep_right(wide_cols_ref[...])

    for u in range(block // RB):
        at = slice(u * RB, (u + 1) * RB)
        first = pl.multiple_of(step * block + u * RB, RB)
        half = half_ref[:, pl.ds(first, RB), :].reshape(rows, 6 * M).astype(BF16)
        slope = jnp.concatenate(
            (own_ref[:, at, :].reshape(rows, width), other_ref[:, at, :].reshape(rows, width)),
            axis=0,
        )
        result = mm(half, wide2_ref[...]) + dot_tall(kron2_ref[...], slope)
        out_ref[:, at, :] = result.reshape(channels, RB, width)


def back_pass(own, other, grid, rows_t, wide_cols, point):
    channels, height, width = own.shape
    args = (own, other, grid, rows_t, wide_cols, point)
    block = pl.BlockSpec((channels, 4 * RB, width), lambda i: (0, i, 0))
    return pl.pallas_call(
        back_kernel,
        grid=(height // (4 * RB),),
        in_specs=[block, block] + [whole(arg.shape) for arg in args[2:]],
        out_specs=block,
        out_shape=jax.ShapeDtypeStruct((channels, height, width), F32),
        scratch_shapes=[
            pltpu.VMEM((channels, height, 6 * M), F32),
            pltpu.VMEM((2 * point.shape[0] * RB, point.shape[1] * RB), BF16),
            pltpu.VMEM((6 * M, width), BF16),
        ],
        compiler_params=pltpu.CompilerParams(vmem_limit_bytes=40 * MIB),
    )(*args)


MESH = pl.DeviceIdType.MESH


def greet_all(n_row, n_col):
    n = n_row * n_col
    barrier = pltpu.get_barrier_semaphore()

    def greet(i, carry):
        pl.semaphore_signal(
            barrier, inc=1, device_id=device_at(n_row, n_col, i // 2, i % 2), device_id_type=MESH
        )
        return carry

    lax.fori_loop(1, 2 * n, greet, 0)
    return barrier


def device_at(n_row, n_col, offset, flip):
    n = n_row * n_col
    at = lax.rem(lax.axis_index("row") * n_col + lax.axis_index("col") + offset, n)
    return (at // n_col, lax.rem(at, n_col), lax.rem(lax.axis_index("ch") + flip, 2))


def send_slices(n_row, n_col, x_ref, landed, send, recv):
    n = n_row * n_col
    me = lax.axis_index("row") * n_col + lax.axis_index("col")

    def copy(k):
        return pltpu.make_async_remote_copy(
            src_ref=x_ref.at[lax.rem(me + k, n)],
            dst_ref=landed.at[k],
            send_sem=send.at[k],
            recv_sem=recv.at[k],
            device_id=device_at(n_row, n_col, k, 0),
            device_id_type=MESH,
        )

    def start(k, carry):
        copy(k).start()
        return carry

    lax.fori_loop(1, n, start, 0)
    return copy


def sum_all(n_row, n_col, x_ref, landed, total, gathered, send1, recv1, send2, recv2):
    n = n_row * n_col
    ch = lax.axis_index("ch")
    me = lax.axis_index("row") * n_col + lax.axis_index("col")
    scatter = send_slices(n_row, n_col, x_ref, landed, send1, recv1)
    total[...] = x_ref[me]

    def take(k, carry):
        scatter(k).wait_recv()
        total[...] += landed[k]
        return carry

    lax.fori_loop(1, n, take, 0)
    gathered[ch * n + me] = total[...]

    def spread(i):
        return pltpu.make_async_remote_copy(
            src_ref=total,
            dst_ref=gathered.at[ch * n + me],
            send_sem=send2.at[i],
            recv_sem=recv2.at[i],
            device_id=device_at(n_row, n_col, i // 2, i % 2),
            device_id_type=MESH,
        )

    def start2(i, carry):
        spread(i).start()
        return carry

    lax.fori_loop(1, 2 * n, start2, 0)

    def end1(k, carry):
        scatter(k).wait_send()
        return carry

    lax.fori_loop(1, n, end1, 0)

    def end2(i, carry):
        spread(i).wait()
        return carry

    lax.fori_loop(1, 2 * n, end2, 0)


def front_kernel(
    n_row, n_col, own, scale, dest_ref, vals_ref, cols_ref, rows_ref, field_ref, got_ref, out_ref,
    held, held_sem, grouped, came, tall_ref, x_ref, landed, total, gathered,
    send0, recv0, send1, recv1, send2, recv2,
):
    n = n_row * n_col
    count, height, width = held.shape[1:]
    cap = grouped.shape[2]
    ch = lax.axis_index("ch")
    me = lax.axis_index("row") * n_col + lax.axis_index("col")
    loads = [
        pltpu.make_async_copy(
            field_ref.at[pl.ds(ch * own + i * count, count)], held.at[i], held_sem.at[i]
        )
        for i in range(own // count)
    ]
    for load in loads:
        load.start()
    barrier = greet_all(n_row, n_col)
    pack(dest_ref[...], vals_ref[...], grouped, n, cap)
    pl.semaphore_wait(barrier, 2 * n - 1)
    trade = send_slices(n_row, n_col, grouped, came, send0, recv0)
    came[0] = grouped[me]

    cols2 = stacked(cols_ref[...], 1)
    for i, load in enumerate(loads):
        load.wait()
        both = mm(stacked(held[i].reshape(count * height, width), 0), cols2)
        half = count * height
        tall = both[:half, : 2 * M] + both[:half, 2 * M :] + both[half:, : 2 * M]
        for c in range(count):
            at = (i * count + c) * M
            tall_ref[:, at : at + M] = tall[c * height : (c + 1) * height, :M]
            at = at + own * M
            tall_ref[:, at : at + M] = tall[c * height : (c + 1) * height, M:]
    lines = jnp.concatenate(mode_lines(rows_ref[...], tall_ref[...], scale), axis=0)
    deep = lines.shape[0] // n
    for p in range(n):
        x_ref[p] = lines[p * deep : (p + 1) * deep]
    sum_all(n_row, n_col, x_ref, landed, total, gathered, send1, recv1, send2, recv2)
    out_ref[...] = gathered[...]

    def end0(k, carry):
        trade(k).wait()
        return carry

    lax.fori_loop(1, n, end0, 0)
    for p in range(n):
        got_ref[:, p * cap : (p + 1) * cap] = came[p]


def front_pass(dest, vals, cols_t, rows, field, own, cap, scale, n_row, n_col):
    n = n_row * n_col
    _, height, width = field.shape
    count = 4
    deep = own * 2 * MODES // 128 // n
    kept = vals.shape[0]
    vmem = pl.BlockSpec(memory_space=pltpu.VMEM)
    got, out = pl.pallas_call(
        functools.partial(front_kernel, n_row, n_col, own, scale),
        out_shape=[
            jax.ShapeDtypeStruct((kept, n * cap), F32),
            jax.ShapeDtypeStruct((2 * n, deep, 128), F32),
        ],
        in_specs=[vmem, vmem, vmem, vmem, pl.BlockSpec(memory_space=pl.ANY)],
        out_specs=[vmem, vmem],
        scratch_shapes=[
            pltpu.VMEM((own // count, count, height, width), F32),
            pltpu.SemaphoreType.DMA((own // count,)),
            pltpu.VMEM((n, kept, cap), F32),
            pltpu.VMEM((n, kept, cap), F32),
            pltpu.VMEM((height, 2 * own * M), F32),
            pltpu.VMEM((n, deep, 128), F32),
            pltpu.VMEM((n, deep, 128), F32),
            pltpu.VMEM((deep, 128), F32),
            pltpu.VMEM((2 * n, deep, 128), F32),
        ]
        + [pltpu.SemaphoreType.DMA((n,))] * 4
        + [pltpu.SemaphoreType.DMA((2 * n,))] * 2,
        compiler_params=pltpu.CompilerParams(
            collective_id=0, has_side_effects=True, vmem_limit_bytes=58 * MIB
        ),
    )(dest, vals, cols_t, rows, field)
    return got, unfold(out.reshape(2, n * deep, 128), own)


def unfold(lines, own):
    wide = 128 // M
    lines = lines.reshape(2, 2, own // wide, A, wide, M).transpose(1, 0, 2, 4, 3, 5)
    return lines.reshape(2, 2 * own, MODES)


def mode_grid(re, im):
    count = re.shape[0]
    re = re.reshape(count, A, M)
    im = im.reshape(count, A, M)
    return jnp.concatenate(
        (jnp.concatenate((re, im), axis=2), jnp.concatenate((-im, re), axis=2)), axis=1
    )


def per_device(
    field, spec_weight, point_weight, bias, kept_modes, residual, trace_dest, trace_cell
):
    n_row = lax.axis_size("row")
    n_col = lax.axis_size("col")
    ch = lax.axis_index("ch")
    inputs, height, width = field.shape
    own = inputs // lax.axis_size("ch")
    first = ch * own
    points = trace_dest.shape[0]
    tiles = n_row * n_col
    points_all = points * tiles
    cap = max(2, 2 * points // tiles)
    forward_scale = 1.0 / math.sqrt(height * n_row * width * n_col)
    mix_scale = 1.0 / math.sqrt(MODES)

    rows = row_table(lax.axis_index("row") * height, height, height * n_row)
    cols = col_table(lax.axis_index("col") * width, width, width * n_col)
    rows_t = rows.T
    cols_t = cols.T
    wide_cols = jnp.concatenate((cols[:M], -cols[M:]), axis=0)

    vals = jnp.concatenate(
        (residual, (trace_cell + 1).astype(F32)[None, :], jnp.zeros((7, points), F32)), axis=0
    )
    got, spec = front_pass(
        trace_dest, vals, cols_t, rows, field, own, cap, forward_scale, n_row, n_col
    )
    spec_re, spec_im = spec[0], spec[1]

    allowed = mode_mask(kept_modes)
    own_allowed = lax.dynamic_slice_in_dim(allowed, first, own, 0)
    out_w = lax.dynamic_slice_in_dim(spec_weight, first, own, 2)
    mixed_re = own_allowed * jnp.sum(
        out_w[0] * spec_re[:, None, :] - out_w[1] * spec_im[:, None, :], axis=0
    )
    mixed_im = own_allowed * jnp.sum(
        out_w[0] * spec_im[:, None, :] + out_w[1] * spec_re[:, None, :], axis=0
    )
    out_point = lax.dynamic_slice_in_dim(point_weight, first, own, 1).T
    slope, other_slope, modes, point_sum = slope_pass(
        field, mode_grid(mixed_re * mix_scale, mixed_im * mix_scale), wide_cols, cols_t, rows,
        rows_t, out_point, jnp.repeat(bias, RB)[:, None], got, mix_scale, n_row, n_col,
    )
    modes_re, modes_im = modes[0], modes[1]
    own_modes = lax.dynamic_slice_in_dim(modes, first, own, 1)
    own_gre, own_gim = own_modes[0], own_modes[1]
    point_lines = inputs * own // 128
    mine = lax.dynamic_slice_in_dim(point_sum, ch, 1, 0)[0, :point_lines]
    norm_points = 1.0 / math.sqrt(points_all)
    grad_point = mine.reshape(inputs, own) * norm_points
    grad_bias = own_gre[:, 0] * (norm_points / mix_scale)

    grad_scale = math.sqrt(MODES / points_all)
    keep_re = own_allowed * own_gre * grad_scale
    keep_im = own_allowed * own_gim * grad_scale
    grad_spec = jnp.stack(
        (
            keep_re[None] * spec_re[:, None] + keep_im[None] * spec_im[:, None],
            keep_im[None] * spec_re[:, None] - keep_re[None] * spec_im[:, None],
        ),
        axis=0,
    )
    in_w = lax.dynamic_slice_in_dim(spec_weight, first, own, 1)
    all_re = allowed * modes_re * forward_scale
    all_im = allowed * modes_im * forward_scale
    adjoint_re = jnp.sum(in_w[0] * all_re[None] + in_w[1] * all_im[None], axis=1)
    adjoint_im = jnp.sum(in_w[0] * all_im[None] - in_w[1] * all_re[None], axis=1)
    own_point = lax.dynamic_slice_in_dim(point_weight, first, own, 0)
    back_point = jnp.concatenate(
        (
            lax.dynamic_slice_in_dim(own_point, first, own, 1),
            lax.dynamic_slice_in_dim(own_point, own - first, own, 1),
        ),
        axis=1,
    )
    grad_field = back_pass(
        slope, other_slope, mode_grid(adjoint_re, adjoint_im), rows_t, wide_cols, back_point
    )
    return (grad_field, grad_spec, grad_point, grad_bias)


def solution(mesh):
    return jax.shard_map(
        per_device,
        mesh=mesh,
        in_specs=(
            P(None, "row", "col"),
            P(),
            P(),
            P("ch"),
            P(),
            P("ch", ("row", "col")),
            P(("row", "col"), None),
            P(("row", "col")),
        ),
        out_specs=(P("ch", "row", "col"), P(None, None, "ch", None), P(None, "ch"), P("ch")),
        check_vma=False,
    )
```

```python
import functools
import math

import jax
import jax.numpy as jnp
from jax import lax
from jax.experimental import pallas as pl
from jax.experimental.pallas import tpu as pltpu
from jax.sharding import PartitionSpec as P

M = 16
A = 2 * M
MODES = A * M
RB = 8
F32 = jnp.float32
BF16 = jnp.bfloat16
FULL_TURN = 6.283185307179586
NN = (((1,), (0,)), ((), ()))
NT = (((1,), (1,)), ((), ()))
MIB = 1 << 20


def row_table(start_at, extent, period):
    frequency = jnp.arange(A, dtype=jnp.int32)
    frequency = jnp.where(frequency < M, frequency, frequency - A)
    places = start_at + jnp.arange(extent, dtype=jnp.int32)
    phases = frequency[:, None] * places[None, :] % period
    angles = phases.astype(F32) * (FULL_TURN / period)
    return jnp.concatenate((jnp.cos(angles), jnp.sin(angles)), axis=0)


def col_table(start_at, extent, period):
    frequency = jnp.arange(M, dtype=jnp.int32)
    places = start_at + jnp.arange(extent, dtype=jnp.int32)
    phases = frequency[:, None] * places[None, :] % period
    angles = phases.astype(F32) * (FULL_TURN / period)
    return jnp.concatenate((jnp.cos(angles), jnp.sin(angles)), axis=0)


def mode_mask(kept_modes):
    indices = jnp.arange(MODES, dtype=jnp.int32)
    row_mode = indices // M
    col_mode = indices % M
    row_rank = jnp.where(row_mode < M, row_mode, 2 * M - 1 - row_mode)
    allowed = (row_rank[None, :] < kept_modes[:, None]) & (col_mode[None, :] < kept_modes[:, None])
    return allowed.astype(F32)


def split2(x):
    hi = x.astype(BF16)
    return hi, (x - hi.astype(F32)).astype(BF16)


def mm(a, b, dims=NN):
    return lax.dot_general(a, b, dims, preferred_element_type=F32)


def dot3(a, b, dims=NN):
    return mm(a[0], b[0], dims) + (mm(a[0], b[1], dims) + mm(a[1], b[0], dims))


def stacked(x, axis):
    hi, low = split2(x)
    return jnp.concatenate((hi.astype(F32), low.astype(F32)), axis=axis).astype(BF16)


def dot_tall(a_stack, b):
    count = a_stack.shape[0] // 2
    hi, low = split2(b)
    both = mm(a_stack, hi)
    return both[:count] + both[count:] + mm(a_stack[:count], low)


def deep_left(x):
    hi = x.astype(BF16).astype(F32)
    return jnp.concatenate((hi, x - hi, hi), axis=1)


def deep_right(x):
    hi = x.astype(BF16).astype(F32)
    return jnp.concatenate((hi, hi, x - hi), axis=0).astype(BF16)


def pack(dest, vals, out_ref, tiles, cap):
    n = dest.shape[0]
    wide = max(tiles, 128)
    named = dest == lax.broadcasted_iota(jnp.int32, (n, wide), 1)
    one_hot = named.astype(F32).astype(BF16)
    before = (
        lax.broadcasted_iota(jnp.int32, (n, n), 1) < lax.broadcasted_iota(jnp.int32, (n, n), 0)
    )
    earlier = mm(before.astype(F32).astype(BF16), one_hot)
    rank = jnp.sum(jnp.where(named, earlier, 0.0), axis=1, keepdims=True)
    position = dest * cap + rank.astype(jnp.int32)
    rows = vals.shape[0]
    hi = vals.astype(BF16)
    left = vals - hi.astype(F32)
    mid = left.astype(BF16)
    low = (left - mid.astype(F32)).astype(BF16)
    parts = jnp.concatenate((hi.astype(F32), mid.astype(F32), low.astype(F32)), axis=0).astype(BF16)
    step = 512
    for first in range(0, tiles * cap, step):
        at = lax.broadcasted_iota(jnp.int32, (n, step), 1) + first
        place = (position == at).astype(F32).astype(BF16)
        got = mm(parts, place)
        got = got[:rows] + got[rows : 2 * rows] + got[2 * rows : 3 * rows]
        for at in range(0, step, cap):
            out_ref[(first + at) // cap] = got[:, at : at + cap]


def mode_lines(rows, tall, scale):
    side = tall.shape[1] // 2
    both = mm(stacked(rows, 0), stacked(tall, 1))
    grid = both[: 2 * A, : 2 * side] + both[2 * A :, : 2 * side] + both[: 2 * A, 2 * side :]
    re = (grid[:A, :side] - grid[A:, side:]) * scale
    im = (grid[A:, :side] + grid[:A, side:]) * (-scale)
    return [part[:, at : at + 128] for part in (re, im) for at in range(0, side, 128)]


def exact(a, b):
    return lax.dot_general(
        a, b, NN, precision=lax.Precision.HIGHEST, preferred_element_type=F32
    )


def iota(shape, axis):
    return lax.broadcasted_iota(jnp.int32, shape, axis)


def spread_rows(weights):
    a, b = weights.shape
    left = (iota((a * RB, a), 0) // RB == iota((a * RB, a), 1)).astype(F32)
    right = (iota((b, b * RB), 1) // RB == iota((b, b * RB), 0)).astype(F32)
    shape = (a * RB, b * RB)
    same = iota(shape, 0) % RB == iota(shape, 1) % RB
    return jnp.where(same, exact(exact(left, weights), right), 0.0)


def slope_kernel(
    n_row, n_col, scale, field_ref, grid_ref, tall_rows_ref, wide_cols_ref, tall_cols_ref,
    rows_ref, point_ref, bias_ref, got_ref,
    slope_ref, other_ref, out_ref,
    half_ref, hot_ref, v_ref, tall_ref, acc_ref, kron2_ref, wide2_ref, cols2_ref, rowid_ref,
    made_ref, swap_send, swap_recv, x_ref, landed, total, gathered, send1, recv1, send2, recv2,
):
    step = pl.program_id(0)
    n = n_row * n_col
    channels, block, width = slope_ref.shape
    steps = made_ref.shape[0]
    rows = channels * RB
    points = got_ref.shape[1]
    inputs = field_ref.shape[0]

    def swap(i):
        return pltpu.make_async_remote_copy(
            src_ref=made_ref.at[i],
            dst_ref=other_ref.at[:, pl.ds(i * block, block), :],
            send_sem=swap_send.at[i],
            recv_sem=swap_recv.at[i],
            device_id=device_at(n_row, n_col, 0, 1),
            device_id_type=MESH,
        )

    @pl.when(step == 0)
    def _():
        greet_all(n_row, n_col)
        tall_rows = deep_left(tall_rows_ref[...]).astype(BF16)
        for o in range(channels):
            half_ref[o] = deep_left(mm(tall_rows, deep_right(grid_ref[o])))
        vals = got_ref[:channels, :]
        hi = vals.astype(BF16).astype(F32)
        both = jnp.concatenate((hi, vals - hi), axis=0)
        both = jnp.broadcast_to(both[:, None, :], (2 * channels, RB, points))
        v_ref[...] = both.reshape(2 * rows, points).astype(BF16)
        cell = got_ref[channels : channels + 1, :].astype(jnp.int32) - 1
        rowid_ref[...] = jnp.where(cell < 0, -1, cell // width)
        colid = jnp.where(cell < 0, -1, cell % width).astype(F32)
        for first in range(0, points, 128):
            ids = jnp.broadcast_to(colid[:, first : first + 128], (128, 128)).T
            for at in range(0, width, 128):
                hot = ids == (iota((128, 128), 1) + at).astype(F32)
                hot_ref[first : first + 128, at : at + 128] = hot.astype(F32).astype(BF16)
        acc_ref[...] = jnp.zeros_like(acc_ref)
        kron2_ref[...] = stacked(spread_rows(point_ref[...]), 0)
        wide2_ref[...] = deep_right(wide_cols_ref[...])
        cols2_ref[...] = stacked(tall_cols_ref[...], 1)

    subs = block // RB
    picked = []
    for u in range(subs):
        first = step * block + u * RB
        here = rowid_ref[...] == first + lax.broadcasted_iota(jnp.int32, (RB, points), 0)
        here = here.astype(F32)
        here = jnp.concatenate((here, here), axis=0).astype(BF16)
        here = jnp.broadcast_to(here[None], (rows // RB, 2 * RB, points)).reshape(2 * rows, points)
        picked.append(v_ref[...] * here)
    cots = mm(jnp.concatenate(picked, axis=0), hot_ref[...])
    k = math.sqrt(2.0 / math.pi)
    fields, slopes = [], []
    for u in range(subs):
        first = pl.multiple_of(step * block + u * RB, RB)
        hi, low = split2(field_ref[:, u * RB : (u + 1) * RB, :].reshape(inputs * RB, width))
        half = half_ref[:, pl.ds(first, RB), :].reshape(rows, 6 * M).astype(BF16)
        both = mm(kron2_ref[...], hi)
        pre = (
            mm(half, wide2_ref[...])
            + (both[:rows] + both[rows:] + mm(kron2_ref[:rows, :], low))
            + bias_ref[...]
        )
        cot = cots[2 * rows * u : 2 * rows * u + rows] + cots[2 * rows * u + rows : 2 * rows * (u + 1)]
        square = pre * pre
        t = jnp.tanh(k * pre * (1.0 + 0.044715 * square))
        rate = 0.5 * (1.0 + t) + 0.5 * k * pre * (1.0 - t * t) * (1.0 + 3 * 0.044715 * square)
        slope = cot * rate
        slope_ref[:, u * RB : (u + 1) * RB, :] = slope.reshape(channels, RB, width)
        made_ref[step, :, u * RB : (u + 1) * RB, :] = slope.reshape(channels, RB, width)
        parts = stacked(slope, 0)
        got = mm(parts, cols2_ref[...])
        tall = got[:rows, : 2 * M] + got[:rows, 2 * M :] + got[rows:, : 2 * M]
        for o in range(channels):
            for part in range(2):
                at = (part * channels + o) * M
                tall_ref[pl.ds(first, RB), at : at + M] = tall[
                    o * RB : (o + 1) * RB, part * M : (part + 1) * M
                ]
        fields.append(jnp.concatenate((hi, low), axis=0))
        slopes.append(parts)
    acc_ref[...] += mm(jnp.concatenate(fields, axis=1), jnp.concatenate(slopes, axis=1), NT)

    @pl.when(step == 0)
    def _():
        pl.semaphore_wait(pltpu.get_barrier_semaphore(), 2 * n - 1)

    swap(step).start()

    @pl.when(step == steps - 1)
    def _():
        lines = mode_lines(rows_ref[...], tall_ref[...], scale)
        total_point = acc_ref[: inputs * RB, :] + acc_ref[inputs * RB :, :]
        total_point = total_point[:, :rows] + total_point[:, rows:]
        same = iota(total_point.shape, 0) % RB == iota(total_point.shape, 1) % RB
        kept = jnp.sum(jnp.where(same, total_point, 0.0).reshape(inputs, RB, rows), axis=1)
        each = 128 // channels
        group = (iota((rows, 128), 0) // RB == iota((rows, 128), 1) % channels).astype(F32)
        wide = exact(kept, group)
        own = iota(wide.shape, 1) // channels == iota(wide.shape, 0) % each
        lines.append(jnp.sum(jnp.where(own, wide, 0.0).reshape(inputs // each, each, 128), axis=1))
        deep = x_ref.shape[1]
        count = sum(line.shape[0] for line in lines)
        lines.append(jnp.zeros((n * deep - count, 128), F32))
        lines = jnp.concatenate(lines, axis=0)
        for p in range(n):
            x_ref[p] = lines[p * deep : (p + 1) * deep]
        sum_all(n_row, n_col, x_ref, landed, total, gathered, send1, recv1, send2, recv2)
        out_ref[...] = gathered[...]

        def end(i, carry):
            swap(i).wait()
            return carry

        lax.fori_loop(0, steps, end, 0)


def whole(shape):
    return pl.BlockSpec(shape, lambda i: (0,) * len(shape))


def slope_pass(
    field, grid, wide_cols, cols_t, rows, rows_t, point, bias, got, scale, n_row, n_col
):
    n = n_row * n_col
    inputs, height, width = field.shape
    channels = grid.shape[0]
    points = got.shape[1]
    lanes = channels * RB
    block = 2 * RB
    steps = height // block
    mode_count = channels * 2 * MODES // 128
    deep = -(-(mode_count + inputs * channels // 128) // n)
    args = (field, grid, rows_t, wide_cols, cols_t, rows, point, bias, got)
    slope, other, out = pl.pallas_call(
        functools.partial(slope_kernel, n_row, n_col, scale),
        grid=(steps,),
        in_specs=[pl.BlockSpec((inputs, block, width), lambda i: (0, i, 0))]
        + [whole(arg.shape) for arg in args[1:]],
        out_specs=[
            pl.BlockSpec((channels, block, width), lambda i: (0, i, 0)),
            pl.BlockSpec(memory_space=pl.ANY),
            whole((2 * n, deep, 128)),
        ],
        out_shape=[
            jax.ShapeDtypeStruct((channels, height, width), F32),
            jax.ShapeDtypeStruct((channels, height, width), F32),
            jax.ShapeDtypeStruct((2 * n, deep, 128), F32),
        ],
        scratch_shapes=[
            pltpu.VMEM((channels, height, 6 * M), F32),
            pltpu.VMEM((points, width), BF16),
            pltpu.VMEM((2 * lanes, points), BF16),
            pltpu.VMEM((height, 2 * channels * M), F32),
            pltpu.VMEM((2 * inputs * RB, 2 * lanes), F32),
            pltpu.VMEM((2 * lanes, inputs * RB), BF16),
            pltpu.VMEM((6 * M, width), BF16),
            pltpu.VMEM((width, 4 * M), BF16),
            pltpu.VMEM((1, points), jnp.int32),
            pltpu.VMEM((steps, channels, block, width), F32),
            pltpu.SemaphoreType.DMA((steps,)),
            pltpu.SemaphoreType.DMA((steps,)),
            pltpu.VMEM((n, deep, 128), F32),
            pltpu.VMEM((n, deep, 128), F32),
            pltpu.VMEM((deep, 128), F32),
            pltpu.VMEM((2 * n, deep, 128), F32),
            pltpu.SemaphoreType.DMA((n,)),
            pltpu.SemaphoreType.DMA((n,)),
            pltpu.SemaphoreType.DMA((2 * n,)),
            pltpu.SemaphoreType.DMA((2 * n,)),
        ],
        compiler_params=pltpu.CompilerParams(
            collective_id=1, has_side_effects=True, vmem_limit_bytes=52 * MIB
        ),
    )(*args)
    out = out.reshape(2, n * deep, 128)
    return slope, other, unfold(out[:, :mode_count], channels), out[:, mode_count:]


def back_kernel(
    own_ref, other_ref, grid_ref, tall_rows_ref, wide_cols_ref, point_ref, out_ref,
    half_ref, kron2_ref, wide2_ref,
):
    step = pl.program_id(0)
    channels, block, width = out_ref.shape
    rows = channels * RB

    @pl.when(step == 0)
    def _():
        tall_rows = deep_left(tall_rows_ref[...]).astype(BF16)
        for c in range(channels):
            half_ref[c] = deep_left(mm(tall_rows, deep_right(grid_ref[c])))
        kron2_ref[...] = stacked(spread_rows(point_ref[...]), 0)
        wide2_ref[...] = deep_right(wide_cols_ref[...])

    for u in range(block // RB):
        at = slice(u * RB, (u + 1) * RB)
        first = pl.multiple_of(step * block + u * RB, RB)
        half = half_ref[:, pl.ds(first, RB), :].reshape(rows, 6 * M).astype(BF16)
        slope = jnp.concatenate(
            (own_ref[:, at, :].reshape(rows, width), other_ref[:, at, :].reshape(rows, width)),
            axis=0,
        )
        result = mm(half, wide2_ref[...]) + dot_tall(kron2_ref[...], slope)
        out_ref[:, at, :] = result.reshape(channels, RB, width)


def back_pass(own, other, grid, rows_t, wide_cols, point):
    channels, height, width = own.shape
    args = (own, other, grid, rows_t, wide_cols, point)
    block = pl.BlockSpec((channels, 4 * RB, width), lambda i: (0, i, 0))
    return pl.pallas_call(
        back_kernel,
        grid=(height // (4 * RB),),
        in_specs=[block, block] + [whole(arg.shape) for arg in args[2:]],
        out_specs=block,
        out_shape=jax.ShapeDtypeStruct((channels, height, width), F32),
        scratch_shapes=[
            pltpu.VMEM((channels, height, 6 * M), F32),
            pltpu.VMEM((2 * point.shape[0] * RB, point.shape[1] * RB), BF16),
            pltpu.VMEM((6 * M, width), BF16),
        ],
        compiler_params=pltpu.CompilerParams(vmem_limit_bytes=52 * MIB),
    )(*args)


MESH = pl.DeviceIdType.MESH


def greet_all(n_row, n_col):
    n = n_row * n_col
    barrier = pltpu.get_barrier_semaphore()

    def greet(i, carry):
        pl.semaphore_signal(
            barrier, inc=1, device_id=device_at(n_row, n_col, i // 2, i % 2), device_id_type=MESH
        )
        return carry

    lax.fori_loop(1, 2 * n, greet, 0)
    return barrier


def device_at(n_row, n_col, offset, flip):
    n = n_row * n_col
    at = lax.rem(lax.axis_index("row") * n_col + lax.axis_index("col") + offset, n)
    return (at // n_col, lax.rem(at, n_col), lax.rem(lax.axis_index("ch") + flip, 2))


def send_slices(n_row, n_col, x_ref, landed, send, recv):
    n = n_row * n_col
    me = lax.axis_index("row") * n_col + lax.axis_index("col")

    def copy(k):
        return pltpu.make_async_remote_copy(
            src_ref=x_ref.at[lax.rem(me + k, n)],
            dst_ref=landed.at[k],
            send_sem=send.at[k],
            recv_sem=recv.at[k],
            device_id=device_at(n_row, n_col, k, 0),
            device_id_type=MESH,
        )

    def start(k, carry):
        copy(k).start()
        return carry

    lax.fori_loop(1, n, start, 0)
    return copy


def sum_all(n_row, n_col, x_ref, landed, total, gathered, send1, recv1, send2, recv2):
    n = n_row * n_col
    ch = lax.axis_index("ch")
    me = lax.axis_index("row") * n_col + lax.axis_index("col")
    scatter = send_slices(n_row, n_col, x_ref, landed, send1, recv1)
    total[...] = x_ref[me]

    def take(k, carry):
        scatter(k).wait_recv()
        total[...] += landed[k]
        return carry

    lax.fori_loop(1, n, take, 0)
    gathered[ch * n + me] = total[...]

    def spread(i):
        return pltpu.make_async_remote_copy(
            src_ref=total,
            dst_ref=gathered.at[ch * n + me],
            send_sem=send2.at[i],
            recv_sem=recv2.at[i],
            device_id=device_at(n_row, n_col, i // 2, i % 2),
            device_id_type=MESH,
        )

    def start2(i, carry):
        spread(i).start()
        return carry

    lax.fori_loop(1, 2 * n, start2, 0)

    def end1(k, carry):
        scatter(k).wait_send()
        return carry

    lax.fori_loop(1, n, end1, 0)

    def end2(i, carry):
        spread(i).wait()
        return carry

    lax.fori_loop(1, 2 * n, end2, 0)


def front_kernel(
    n_row, n_col, own, scale, dest_ref, vals_ref, cols_ref, rows_ref, field_ref, got_ref, out_ref,
    held, held_sem, grouped, came, tall_ref, x_ref, landed, total, gathered,
    send0, recv0, send1, recv1, send2, recv2,
):
    n = n_row * n_col
    count, height, width = held.shape[1:]
    cap = grouped.shape[2]
    ch = lax.axis_index("ch")
    me = lax.axis_index("row") * n_col + lax.axis_index("col")
    loads = [
        pltpu.make_async_copy(
            field_ref.at[pl.ds(ch * own + i * count, count)], held.at[i], held_sem.at[i]
        )
        for i in range(own // count)
    ]
    for load in loads:
        load.start()
    barrier = greet_all(n_row, n_col)
    pack(dest_ref[...], vals_ref[...], grouped, n, cap)
    pl.semaphore_wait(barrier, 2 * n - 1)
    trade = send_slices(n_row, n_col, grouped, came, send0, recv0)
    came[0] = grouped[me]

    cols2 = stacked(cols_ref[...], 1)
    for i, load in enumerate(loads):
        load.wait()
        both = mm(stacked(held[i].reshape(count * height, width), 0), cols2)
        half = count * height
        tall = both[:half, : 2 * M] + both[:half, 2 * M :] + both[half:, : 2 * M]
        for c in range(count):
            at = (i * count + c) * M
            tall_ref[:, at : at + M] = tall[c * height : (c + 1) * height, :M]
            at = at + own * M
            tall_ref[:, at : at + M] = tall[c * height : (c + 1) * height, M:]
    lines = jnp.concatenate(mode_lines(rows_ref[...], tall_ref[...], scale), axis=0)
    deep = lines.shape[0] // n
    for p in range(n):
        x_ref[p] = lines[p * deep : (p + 1) * deep]
    sum_all(n_row, n_col, x_ref, landed, total, gathered, send1, recv1, send2, recv2)
    out_ref[...] = gathered[...]

    def end0(k, carry):
        trade(k).wait()
        return carry

    lax.fori_loop(1, n, end0, 0)
    for p in range(n):
        got_ref[:, p * cap : (p + 1) * cap] = came[p]


def front_pass(dest, vals, cols_t, rows, field, own, cap, scale, n_row, n_col):
    n = n_row * n_col
    _, height, width = field.shape
    count = 4
    deep = own * 2 * MODES // 128 // n
    kept = vals.shape[0]
    vmem = pl.BlockSpec(memory_space=pltpu.VMEM)
    got, out = pl.pallas_call(
        functools.partial(front_kernel, n_row, n_col, own, scale),
        out_shape=[
            jax.ShapeDtypeStruct((kept, n * cap), F32),
            jax.ShapeDtypeStruct((2 * n, deep, 128), F32),
        ],
        in_specs=[vmem, vmem, vmem, vmem, pl.BlockSpec(memory_space=pl.ANY)],
        out_specs=[vmem, vmem],
        scratch_shapes=[
            pltpu.VMEM((own // count, count, height, width), F32),
            pltpu.SemaphoreType.DMA((own // count,)),
            pltpu.VMEM((n, kept, cap), F32),
            pltpu.VMEM((n, kept, cap), F32),
            pltpu.VMEM((height, 2 * own * M), F32),
            pltpu.VMEM((n, deep, 128), F32),
            pltpu.VMEM((n, deep, 128), F32),
            pltpu.VMEM((deep, 128), F32),
            pltpu.VMEM((2 * n, deep, 128), F32),
        ]
        + [pltpu.SemaphoreType.DMA((n,))] * 4
        + [pltpu.SemaphoreType.DMA((2 * n,))] * 2,
        compiler_params=pltpu.CompilerParams(
            collective_id=0, has_side_effects=True, vmem_limit_bytes=52 * MIB
        ),
    )(dest, vals, cols_t, rows, field)
    return got, unfold(out.reshape(2, n * deep, 128), own)


def unfold(lines, own):
    wide = 128 // M
    lines = lines.reshape(2, 2, own // wide, A, wide, M).transpose(1, 0, 2, 4, 3, 5)
    return lines.reshape(2, 2 * own, MODES)


def mode_grid(re, im):
    count = re.shape[0]
    re = re.reshape(count, A, M)
    im = im.reshape(count, A, M)
    return jnp.concatenate(
        (jnp.concatenate((re, im), axis=2), jnp.concatenate((-im, re), axis=2)), axis=1
    )


def per_device(
    field, spec_weight, point_weight, bias, kept_modes, residual, trace_dest, trace_cell
):
    n_row = lax.axis_size("row")
    n_col = lax.axis_size("col")
    ch = lax.axis_index("ch")
    inputs, height, width = field.shape
    own = inputs // lax.axis_size("ch")
    first = ch * own
    points = trace_dest.shape[0]
    tiles = n_row * n_col
    points_all = points * tiles
    cap = max(2, 2 * points // tiles)
    forward_scale = 1.0 / math.sqrt(height * n_row * width * n_col)
    mix_scale = 1.0 / math.sqrt(MODES)

    rows = row_table(lax.axis_index("row") * height, height, height * n_row)
    cols = col_table(lax.axis_index("col") * width, width, width * n_col)
    rows_t = rows.T
    cols_t = cols.T
    wide_cols = jnp.concatenate((cols[:M], -cols[M:]), axis=0)

    vals = jnp.concatenate(
        (residual, (trace_cell + 1).astype(F32)[None, :], jnp.zeros((7, points), F32)), axis=0
    )
    got, spec = front_pass(
        trace_dest, vals, cols_t, rows, field, own, cap, forward_scale, n_row, n_col
    )
    spec_re, spec_im = spec[0], spec[1]

    allowed = mode_mask(kept_modes)
    own_allowed = lax.dynamic_slice_in_dim(allowed, first, own, 0)
    out_w = lax.dynamic_slice_in_dim(spec_weight, first, own, 2)
    mixed_re = own_allowed * jnp.sum(
        out_w[0] * spec_re[:, None, :] - out_w[1] * spec_im[:, None, :], axis=0
    )
    mixed_im = own_allowed * jnp.sum(
        out_w[0] * spec_im[:, None, :] + out_w[1] * spec_re[:, None, :], axis=0
    )
    out_point = lax.dynamic_slice_in_dim(point_weight, first, own, 1).T
    slope, other_slope, modes, point_sum = slope_pass(
        field, mode_grid(mixed_re * mix_scale, mixed_im * mix_scale), wide_cols, cols_t, rows,
        rows_t, out_point, jnp.repeat(bias, RB)[:, None], got, mix_scale, n_row, n_col,
    )
    modes_re, modes_im = modes[0], modes[1]
    own_modes = lax.dynamic_slice_in_dim(modes, first, own, 1)
    own_gre, own_gim = own_modes[0], own_modes[1]
    point_lines = inputs * own // 128
    mine = lax.dynamic_slice_in_dim(point_sum, ch, 1, 0)[0, :point_lines]
    norm_points = 1.0 / math.sqrt(points_all)
    grad_point = mine.reshape(inputs, own) * norm_points
    grad_bias = own_gre[:, 0] * (norm_points / mix_scale)

    grad_scale = math.sqrt(MODES / points_all)
    keep_re = own_allowed * own_gre * grad_scale
    keep_im = own_allowed * own_gim * grad_scale
    grad_spec = jnp.stack(
        (
            keep_re[None] * spec_re[:, None] + keep_im[None] * spec_im[:, None],
            keep_im[None] * spec_re[:, None] - keep_re[None] * spec_im[:, None],
        ),
        axis=0,
    )
    in_w = lax.dynamic_slice_in_dim(spec_weight, first, own, 1)
    all_re = allowed * modes_re * forward_scale
    all_im = allowed * modes_im * forward_scale
    adjoint_re = jnp.sum(in_w[0] * all_re[None] + in_w[1] * all_im[None], axis=1)
    adjoint_im = jnp.sum(in_w[0] * all_im[None] - in_w[1] * all_re[None], axis=1)
    own_point = lax.dynamic_slice_in_dim(point_weight, first, own, 0)
    back_point = jnp.concatenate(
        (
            lax.dynamic_slice_in_dim(own_point, first, own, 1),
            lax.dynamic_slice_in_dim(own_point, own - first, own, 1),
        ),
        axis=1,
    )
    grad_field = back_pass(
        slope, other_slope, mode_grid(adjoint_re, adjoint_im), rows_t, wide_cols, back_point
    )
    return (grad_field, grad_spec, grad_point, grad_bias)


def solution(mesh):
    return jax.shard_map(
        per_device,
        mesh=mesh,
        in_specs=(
            P(None, "row", "col"),
            P(),
            P(),
            P("ch"),
            P(),
            P("ch", ("row", "col")),
            P(("row", "col"), None),
            P(("row", "col")),
        ),
        out_specs=(P("ch", "row", "col"), P(None, None, "ch", None), P(None, "ch"), P("ch")),
        check_vma=False,
    )
```
